32 devices in a mesh: dp: 4 (over z), seq: 8 (over y, x, core).
Axes of the slice: x: 2, y: 2, z: 4, core: 2. Of those that a mesh axis runs over, the one named last changes fastest.
Arguments:
- queries: bfloat16 [4, 1024, 2048], P('dp', 'seq'), may hold values from -34 to 34
- key_rows: bfloat16 [4, 1024, 2048], P('dp', 'seq'), may hold values from -34 to 34
- values: bfloat16 [4, 1024, 2048], P('dp', 'seq'), may hold values from -6 to 6
- adjacency: int32 [4, 8, 8], P('dp'), may hold values from 0 to 7, as said below
- counts: int32 [4, 8], P('dp'), may hold values from 1 to 8, as said below
- out_weight: bfloat16 [2048, 2048], P('dp'), may hold values from -0.125 to 0.125
- out_cotangent: bfloat16 [4, 1024, 2048], P('dp', 'seq'), may hold values from -6 to 6
Outputs:
- layer_out: bfloat16 [4, 1024, 2048], P('dp', 'seq')
- query_grad: bfloat16 [4, 1024, 2048], P('dp', 'seq')
- key_grad: bfloat16 [4, 1024, 2048], P('dp', 'seq')
- value_grad: bfloat16 [4, 1024, 2048], P('dp', 'seq')
- weight_grad: float32 [2048, 2048], P(('dp', 'seq'))
The draws below stay inside these ranges and needn't reach their ends.
Inputs may be any that keep to these rules, and one draw needn't show every extreme that they name: `adjacency`: row i of a sequence lists 8 different key blocks, slot 0 being block i itself; slots at or beyond the row's count are not attended. `counts`: block 0 of every sequence has all 8 slots live.
All inputs are finite; a program needn't handle non-finite values.
Results may differ from the reference program's by a relative error of at most 0.025.
Values may be sent and summed in bfloat16 or wider, within the bound.
No kernel may reach another device: no remote copies, remote signals or barrier semaphores. Data moves between devices by JAX's collectives and lax.ppermute only.
A program may use at most 128 MiB of HBM per device.

```python
import jax
import jax.numpy as jnp
from jax import lax

D = 2048
H = 16
HD = 128
BLK = 128
NBR = 8
SEQS = 4
LEN = 1024
NBLK = 8


def paired(key):
    base = jax.random.fold_in(key, 11)
    first, second = jax.random.split(base, 2)
    shape = (SEQS, LEN, D)
    query_draw = 1.6 * jnp.clip(jax.random.normal(first, shape, jnp.float32), -6.0, 6.0)
    key_draw = 1.6 * jnp.clip(jax.random.normal(second, shape, jnp.float32), -6.0, 6.0)
    return (query_draw, key_draw)


def graph(key):
    base = jax.random.fold_in(key, 29)
    count_key, order_key = jax.random.split(base)
    live = jax.random.randint(count_key, (SEQS, NBLK), 1, NBR + 1)
    live = live.at[:, 0].set(NBR)
    row_keys = jax.random.split(order_key, SEQS * NBLK)
    offsets = jax.vmap(lambda row_key: jax.random.permutation(row_key, NBLK - 1)[:NBR - 1])(row_keys)
    own_block = jnp.arange(SEQS * NBLK) % NBLK
    others = (own_block[:, None] + 1 + offsets) % NBLK
    links = jnp.concatenate([own_block[:, None], others], axis=1).reshape(SEQS, NBLK, NBR)
    return (links.astype(jnp.int32), live.astype(jnp.int32))


def draw_queries(key, part):
    return paired(key)[0].astype(jnp.bfloat16)


def draw_key_rows(key, part):
    return paired(key)[1].astype(jnp.bfloat16)


def draw_adjacency(key, part):
    return graph(key)[0]


def draw_counts(key, part):
    return graph(key)[1]


def block_scale(stream_key, dims, shards, least, top_value):
    level = 1.0
    for dim, shards_of in shards:
        draws = jax.random.uniform(jax.random.fold_in(jax.random.fold_in(stream_key, 6), dim), (shards_of,), jnp.float32, least / len(shards), top_value / len(shards))
        level = level * jnp.repeat(jnp.exp(draws), dims[dim] // shards_of).reshape((-1,) + (1,) * (len(dims) - 1 - dim))
    return level


def scatter_about(stream_key, dims, spread, limit, pieces=(), dtype=jnp.bfloat16):
    drawn = spread * jax.random.normal(stream_key, dims, jnp.float32)
    if pieces:
        drawn = drawn * block_scale(stream_key, dims, pieces, -0.22, 0.18)
    return jnp.clip(drawn, -limit, limit).astype(dtype)


def setup_inputs(seed: int = 0) -> dict:
    seeds = jax.random.split(jax.random.key(seed), 8)
    queries = draw_queries(jax.random.fold_in(seeds[7], 71), 0)
    key_rows = draw_key_rows(jax.random.fold_in(seeds[7], 71), 0)
    values = scatter_about(seeds[2], (SEQS, LEN, D), 1.0, 6.0, ((0, 4), (1, 8)))
    adjacency = draw_adjacency(jax.random.fold_in(seeds[7], 71), 0)
    counts = draw_counts(jax.random.fold_in(seeds[7], 71), 0)
    out_weight = scatter_about(seeds[5], (D, D), D ** -0.5, 0.125, ((0, 4),))
    out_cotangent = scatter_about(seeds[6], (SEQS, LEN, D), 1.0, 6.0, ((0, 4), (1, 8)))
    return {"queries": queries, "key_rows": key_rows, "values": values, "adjacency": adjacency, "counts": counts, "out_weight": out_weight, "out_cotangent": out_cotangent}


def attend(query_blk, key_blk, value_blk, links, live_count):
    scale = HD ** -0.5
    heads = query_blk.shape[2]
    key_near = key_blk[links].reshape(NBLK, NBR * BLK, heads, HD)
    value_near = value_blk[links].reshape(NBLK, NBR * BLK, heads, HD)
    scores = jnp.einsum("iqhd,ikhd->hiqk", query_blk.astype(jnp.float32), key_near.astype(jnp.float32)) * scale
    live = (jnp.arange(NBR * BLK) // BLK)[None, :] < live_count[:, None]
    scores = jnp.where(live[None, :, None, :], scores, -1e30)
    highest = jnp.max(scores, axis=-1, keepdims=True)
    expo = jnp.exp(scores - highest)
    prob = expo / jnp.sum(expo, axis=-1, keepdims=True)
    prob_bf = prob.astype(jnp.bfloat16)
    attended = jnp.einsum("hiqk,ikhd->iqhd", prob_bf.astype(jnp.float32), value_near.astype(jnp.float32)).astype(jnp.bfloat16)
    return prob, prob_bf, attended, key_near, value_near


def backward(query_blk, key_blk, value_blk, links, live_count, grad_blk):
    scale = HD ** -0.5
    heads = query_blk.shape[2]
    prob, prob_bf, attended, key_near, value_near = attend(query_blk, key_blk, value_blk, links, live_count)
    grad_f = grad_blk.astype(jnp.float32)
    value_part = jnp.einsum("hiqk,iqhd->ikhd", prob_bf.astype(jnp.float32), grad_f)
    grad_prob = jnp.einsum("iqhd,ikhd->hiqk", grad_f, value_near.astype(jnp.float32))
    delta = jnp.einsum("iqhd,iqhd->hiq", grad_f, attended.astype(jnp.float32))
    score_grad = (prob * (grad_prob - delta[..., None]) * scale).astype(jnp.bfloat16)
    query_grad = jnp.einsum("hiqk,ikhd->iqhd", score_grad.astype(jnp.float32), key_near.astype(jnp.float32)).astype(jnp.bfloat16)
    key_part = jnp.einsum("hiqk,iqhd->ikhd", score_grad.astype(jnp.float32), query_blk.astype(jnp.float32))
    flat = links.reshape(-1)
    empty = jnp.zeros((NBLK, BLK, heads, HD), jnp.float32)
    key_grad = empty.at[flat].add(key_part.reshape(NBLK * NBR, BLK, heads, HD)).astype(jnp.bfloat16)
    value_grad = empty.at[flat].add(value_part.reshape(NBLK * NBR, BLK, heads, HD)).astype(jnp.bfloat16)
    return query_grad, key_grad, value_grad


def blocks_of(tokens):
    return tokens.reshape(NBLK, BLK, H, HD)


def reference(queries, key_rows, values, adjacency, counts, out_weight, out_cotangent):
    def forward_one(items):
        query_tok, key_tok, value_tok, links, live_count = items
        attended = attend(blocks_of(query_tok), blocks_of(key_tok), blocks_of(value_tok), links, live_count)[2]
        return attended.reshape(LEN, D)

    attn = lax.map(forward_one, (queries, key_rows, values, adjacency, counts))
    flat_attn = attn.reshape(SEQS * LEN, D)
    flat_cot = out_cotangent.reshape(SEQS * LEN, D)
    layer_out = jnp.dot(flat_attn, out_weight, preferred_element_type=jnp.float32).astype(jnp.bfloat16).reshape(SEQS, LEN, D)
    grad_attn = lax.dot_general(flat_cot, out_weight, (((1,), (1,)), ((), ())), preferred_element_type=jnp.float32)
    grad_attn = grad_attn.astype(jnp.bfloat16).reshape(SEQS, LEN, D)
    weight_grad = lax.dot_general(flat_attn, flat_cot, (((0,), (0,)), ((), ())), preferred_element_type=jnp.float32)

    def backward_one(items):
        query_tok, key_tok, value_tok, links, live_count, grad_tok = items
        grads = backward(blocks_of(query_tok), blocks_of(key_tok), blocks_of(value_tok), links, live_count, blocks_of(grad_tok))
        return tuple(part.reshape(LEN, D) for part in grads)

    query_grad, key_grad, value_grad = lax.map(backward_one, (queries, key_rows, values, adjacency, counts, grad_attn))
    return layer_out, query_grad, key_grad, value_grad, weight_grad
```

```python
import functools

import jax
import jax.numpy as jnp
from jax import lax
from jax.experimental import pallas as pl
from jax.experimental.pallas import tpu as pltpu
from jax.sharding import PartitionSpec as P

HD = 128
BLK = 128
NBR = 8
F32 = jnp.float32
BF16 = jnp.bfloat16
NN = (((1,), (0,)), ((), ()))
NT = (((1,), (1,)), ((), ()))
TN = (((0,), (0,)), ((), ()))
LOG2E = 1.4426950408889634
DEAD = -1e30
VMEM = pl.BlockSpec(memory_space=pltpu.VMEM)
SMEM = pl.BlockSpec(memory_space=pltpu.SMEM)
ANY = pl.BlockSpec(memory_space=pl.ANY)
MIB = 1 << 20


def mm(a, b, dims=NN):
    return lax.dot_general(a, b, dims, preferred_element_type=F32)


def sds(shape, dtype):
    return jax.ShapeDtypeStruct(shape, dtype)


def call(kernel, ins, outs, scratch=(), flops=0, moved=0, vmem=24):
    specs = [spec for spec, _ in ins]
    return pl.pallas_call(
        kernel,
        out_shape=tuple(shape for _, shape in outs),
        in_specs=specs,
        out_specs=tuple(spec for spec, _ in outs),
        scratch_shapes=list(scratch),
        compiler_params=pltpu.CompilerParams(vmem_limit_bytes=vmem * MIB),
        cost_estimate=pl.CostEstimate(flops=flops, bytes_accessed=moved, transcendentals=0),
    )(*[arg for _, arg in ins])


def col_of(dev, g, pairs, per):
    core = dev % 2
    return pl.multiple_of(((core * per + g) * pairs + dev // 2) * HD, HD)


def copies(pairs_of_refs, sems):
    handles = [pltpu.make_async_copy(src, dst, sems.at[n]) for n, (src, dst) in enumerate(pairs_of_refs)]
    for handle in handles:
        handle.start()
    for handle in handles:
        handle.wait()


def attend(query_blk, key_blk, value_blk, links, live_count):
    scale = HD ** (-0.5)
    blocks = query_blk.shape[0]
    heads = query_blk.shape[2]
    key_near = key_blk[links].reshape(blocks, NBR * BLK, heads, HD)
    value_near = value_blk[links].reshape(blocks, NBR * BLK, heads, HD)
    scores = (
        jnp.einsum("iqhd,ikhd->hiqk", query_blk, key_near, preferred_element_type=jnp.float32)
        * scale
    )
    live = (jnp.arange(NBR * BLK) // BLK)[None, :] < live_count[:, None]
    scores = jnp.where(live[None, :, None, :], scores, -1e30)
    highest = jnp.max(scores, axis=-1, keepdims=True)
    expo = jnp.exp(scores - highest)
    prob = expo / jnp.sum(expo, axis=-1, keepdims=True)
    prob_bf = prob.astype(jnp.bfloat16)
    attended = jnp.einsum(
        "hiqk,ikhd->iqhd", prob_bf, value_near, preferred_element_type=jnp.float32
    ).astype(jnp.bfloat16)
    return (prob, prob_bf, attended, key_near, value_near)


def backward(query_blk, links, grad_blk, prob, prob_bf, attended, key_near, value_near):
    scale = HD ** (-0.5)
    blocks = query_blk.shape[0]
    heads = query_blk.shape[2]
    value_part = jnp.einsum(
        "hiqk,iqhd->ikhd", prob_bf, grad_blk, preferred_element_type=jnp.float32
    )
    grad_prob = jnp.einsum(
        "iqhd,ikhd->hiqk", grad_blk, value_near, preferred_element_type=jnp.float32
    )
    delta = jnp.einsum("iqhd,iqhd->hiq", grad_blk, attended, preferred_element_type=jnp.float32)
    score_grad = (prob * (grad_prob - delta[..., None]) * scale).astype(jnp.bfloat16)
    query_grad = jnp.einsum(
        "hiqk,ikhd->iqhd", score_grad, key_near, preferred_element_type=jnp.float32
    ).astype(jnp.bfloat16)
    key_part = jnp.einsum(
        "hiqk,iqhd->ikhd", score_grad, query_blk, preferred_element_type=jnp.float32
    )
    member = (links.reshape(-1)[None, :] == jnp.arange(blocks)[:, None]).astype(jnp.float32)
    key_grad = jnp.einsum(
        "ja,aqhd->jqhd",
        member,
        key_part.reshape(blocks * NBR, BLK, heads, HD),
        precision=lax.Precision.HIGHEST,
    )
    value_grad = jnp.einsum(
        "ja,aqhd->jqhd",
        member,
        value_part.reshape(blocks * NBR, BLK, heads, HD),
        precision=lax.Precision.HIGHEST,
    )
    return (query_grad, key_grad.astype(jnp.bfloat16), value_grad.astype(jnp.bfloat16))


def local(queries, key_rows, values, adjacency, counts, out_weight, out_cotangent):
    query_heads, key_heads, value_heads = (
        lax.all_to_all(queries[0], "seq", split_axis=1, concat_axis=0, tiled=True),
        lax.all_to_all(key_rows[0], "seq", split_axis=1, concat_axis=0, tiled=True),
        lax.all_to_all(values[0], "seq", split_axis=1, concat_axis=0, tiled=True),
    )
    length = query_heads.shape[0]
    blocks = length // BLK
    heads = query_heads.shape[1] // HD
    shape = (blocks, BLK, heads, HD)
    links = adjacency[0]
    live_count = counts[0]
    query_blk = query_heads.reshape(shape)
    prob, prob_bf, attended, key_near, value_near = attend(
        query_blk, key_heads.reshape(shape), value_heads.reshape(shape), links, live_count
    )
    attn_tokens = lax.all_to_all(
        attended.reshape(length, heads * HD), "seq", split_axis=0, concat_axis=1, tiled=True
    )
    cotangent = out_cotangent[0]
    columns = attn_tokens
    layer_out = jnp.dot(
        columns,
        lax.all_gather(out_weight, "dp", axis=0, tiled=True),
        preferred_element_type=jnp.float32,
    )
    grad_tokens = lax.dot_general(
        cotangent,
        lax.all_gather(out_weight, "dp", axis=0, tiled=True),
        (((1,), (1,)), ((), ())),
        preferred_element_type=jnp.float32,
    )
    grad_heads = lax.all_to_all(
        grad_tokens.astype(jnp.bfloat16), "seq", split_axis=1, concat_axis=0, tiled=True
    )
    query_grad, key_grad, value_grad = backward(
        query_blk, links, grad_heads.reshape(shape), prob, prob_bf, attended, key_near, value_near
    )
    query_back, key_back, value_back = (
        lax.all_to_all(
            query_grad.reshape(length, heads * HD), "seq", split_axis=0, concat_axis=1, tiled=True
        ),
        lax.all_to_all(
            key_grad.reshape(length, heads * HD), "seq", split_axis=0, concat_axis=1, tiled=True
        ),
        lax.all_to_all(
            value_grad.reshape(length, heads * HD), "seq", split_axis=0, concat_axis=1, tiled=True
        ),
    )
    columns = attn_tokens
    weight_grad = lax.psum_scatter(
        lax.dot_general(
            columns, cotangent, (((0,), (0,)), ((), ())), preferred_element_type=jnp.float32
        ),
        ("dp", "seq"),
        scatter_dimension=0,
        tiled=True,
    )
    return (
        layer_out.astype(jnp.bfloat16)[None],
        query_back[None],
        key_back[None],
        value_back[None],
        weight_grad,
    )


def prep_kernel(n, per, q_ref, k_ref, v_ref, c_ref, w_ref, *rest):
    qkv, (same, other, wsend, sems) = rest[:n], rest[n:]
    s = lax.axis_index("seq")
    core = s % 2
    half = c_ref.shape[2] // 2
    moves = []
    for j in range(n):
        dev = s ^ j
        for t, src in enumerate((q_ref, k_ref, v_ref)):
            for g in range(per):
                col = col_of(dev, g, n // 2, per)
                moves.append((src.at[0, :, pl.ds(col, HD)], qkv[j].at[t, :, pl.ds(g * HD, HD)]))
    mine = pl.multiple_of(core * half, half)
    theirs = pl.multiple_of((1 - core) * half, half)
    moves.append((c_ref.at[0, :, pl.ds(mine, half)], same))
    moves.append((c_ref.at[0, :, pl.ds(theirs, half)], other))
    row = pl.multiple_of((s // 2) * HD, HD)
    moves.append((w_ref.at[pl.ds(row, HD), pl.ds(mine, half)], wsend))
    copies(moves, sems)


def forward_kernel(n, per, adj_ref, cnt_ref, *rest):
    qkv = rest[:n]
    attn_ref, swap_ref, attn_t_ref, lse_ref, bias_ref = rest[n : n + 5]
    keys, vals_t, score, expo = rest[n + 5 :]
    s = lax.axis_index("seq")
    length = n * BLK
    scale = HD**-0.5 * LOG2E
    place = lax.broadcasted_iota(jnp.int32, (n, BLK), 0)
    for i in range(n):
        block = s ^ i
        count = cnt_ref[0, block]
        bias = jnp.full((n, BLK), DEAD, F32)
        for slot in range(NBR):
            j = jnp.where(slot < count, adj_ref[0, block, slot] ^ s, n)
            bias = jnp.where(place == j, 0.0, bias)
        bias_ref[:, i * BLK : (i + 1) * BLK] = bias
    tile = 2 * BLK
    for g in range(per):
        lanes = slice(g * HD, (g + 1) * HD)
        for j in range(n):
            rows = slice(j * BLK, (j + 1) * BLK)
            keys[g, rows, :] = qkv[j][1, :, lanes]
            vals_t[g, :, rows] = qkv[j][2, :, lanes].T
        for t in range(length // tile):
            cols = slice(t * tile, (t + 1) * tile)
            query = jnp.concatenate([qkv[2 * t][0, :, lanes], qkv[2 * t + 1][0, :, lanes]], axis=0)
            highest = jnp.full((1, tile), -jnp.inf, F32)
            for j in range(n):
                rows = slice(j * BLK, (j + 1) * BLK)
                part = mm(keys[g, rows, :], query, NT) * scale + bias_ref[j : j + 1, cols]
                score[rows, :] = part
                highest = jnp.maximum(highest, jnp.max(part, axis=0, keepdims=True))
            total = jnp.zeros((1, tile), F32)
            for j in range(n):
                rows = slice(j * BLK, (j + 1) * BLK)
                part = jnp.exp2(score[rows, :] - highest)
                total = total + jnp.sum(part, axis=0, keepdims=True)
                expo[rows, :] = part.astype(BF16)
            att = (mm(vals_t[g], expo[...]) * (1.0 / total)).astype(BF16)
            attn_t_ref[g, :, cols] = att
            lse_ref[g : g + 1, cols] = highest + jnp.log2(total)
            first, second = att[:, :BLK].T, att[:, BLK:].T
            base = t * tile
            attn_ref[base : base + BLK, lanes] = first
            attn_ref[base + BLK : base + tile, lanes] = second
            swap_ref[base : base + BLK, lanes] = second
            swap_ref[base + BLK : base + tile, lanes] = first


def grad_attn_kernel(n, per, *rest):
    cot = rest[:n]
    wts = rest[n : n + 2 * per]
    own_ref, send_ref, w_out, cot_out = rest[n + 2 * per :]
    core = lax.axis_index("seq") % 2
    z = lax.axis_index("dp")
    for jz in range(2 * per):
        slot = (z ^ jz) ^ (per * core)
        w_out[pl.ds(pl.multiple_of(slot * HD, HD), HD), :] = wts[jz][...]
    for j in range(n):
        cot_out[j * BLK : (j + 1) * BLK, :] = cot[j][...]
    mine = per * HD
    for t in range(n // 2):
        base = 2 * t * BLK
        part = mm(w_out[...], cot_out[base : base + 2 * BLK, :], NT)
        own_ref[:, base : base + 2 * BLK] = part[:mine]
        send_ref[:, base : base + BLK] = part[mine:, BLK:].astype(BF16)
        send_ref[:, base + BLK : base + 2 * BLK] = part[mine:, :BLK].astype(BF16)


def backward_kernel(n, per, *rest):
    qkv = rest[:n]
    attn_t_ref, lse_ref, bias_ref, own_ref, recv_ref = rest[n : n + 5]
    outs = rest[n + 5 : 2 * n + 5]
    queries, keys_t, grad, delta, probs, dscores, dq_t = rest[2 * n + 5 :]
    scale = HD**-0.5
    tile = 2 * BLK
    length = n * BLK
    for g in range(per):
        lanes = slice(g * HD, (g + 1) * HD)
        grad_t = (own_ref[lanes, :] + recv_ref[lanes, :].astype(F32)).astype(BF16)
        grad[g] = grad_t
        delta[g : g + 1, :] = jnp.sum(
            grad_t.astype(F32) * attn_t_ref[g].astype(F32), axis=0, keepdims=True
        )
        for j in range(n):
            rows = slice(j * BLK, (j + 1) * BLK)
            queries[g, rows, :] = qkv[j][0, :, lanes]
            keys_t[g, :, rows] = qkv[j][1, :, lanes].T
        for t in range(length // tile):
            key = jnp.concatenate([qkv[2 * t][1, :, lanes], qkv[2 * t + 1][1, :, lanes]], axis=0)
            value = jnp.concatenate([qkv[2 * t][2, :, lanes], qkv[2 * t + 1][2, :, lanes]], axis=0)
            for u in range(length // tile):
                cols = slice(u * tile, (u + 1) * tile)
                score = mm(key, queries[g, cols, :], NT)
                dprob = mm(value, grad[g, :, cols])
                lse = lse_ref[g : g + 1, cols]
                dlt = delta[g : g + 1, cols]
                for b in range(2):
                    rows = slice(b * BLK, (b + 1) * BLK)
                    shift = bias_ref[2 * t + b : 2 * t + b + 1, cols] - lse
                    prob = jnp.exp2(score[rows] * (scale * LOG2E) + shift)
                    probs[rows, cols] = prob.astype(BF16)
                    dscores[rows, cols] = (prob * (dprob[rows] - dlt)).astype(BF16)
            dvalue = mm(probs[...], grad[g], NT).astype(BF16)
            dkey = (mm(dscores[...], queries[g]) * scale).astype(BF16)
            for b in range(2):
                rows = slice(b * BLK, (b + 1) * BLK)
                outs[2 * t + b][1, :, lanes] = dkey[rows]
                outs[2 * t + b][2, :, lanes] = dvalue[rows]
            part = mm(keys_t[g, :, t * tile : (t + 1) * tile], dscores[...])
            if t == 0:
                dq_t[...] = part
            else:
                dq_t[...] += part
        for j in range(n):
            rows = slice(j * BLK, (j + 1) * BLK)
            outs[j][0, :, lanes] = (dq_t[:, rows].T * scale).astype(BF16)


def out_kernel(n, attn_ref, recv_ref, w_ref, *outs):
    tile = 2 * BLK
    half = attn_ref.shape[1]
    for t in range(n // 2):
        rows = slice(t * tile, (t + 1) * tile)
        part = mm(attn_ref[rows, :], w_ref[:half, :]) + mm(recv_ref[rows, :], w_ref[half:, :])
        outs[t][...] = part.astype(outs[t].dtype)


def weight_kernel(nz, attn_t_ref, recv_ref, cot_ref, *rest):
    outs, grads = rest[:nz], rest[nz]
    core = lax.axis_index("seq") % 2
    z = lax.axis_index("dp")
    per = nz // 2
    for g in range(per):
        grads[g] = mm(attn_t_ref[g], cot_ref[...])
        recv = recv_ref[:, g * HD : (g + 1) * HD].T
        grads[per + g] = mm(recv, cot_ref[...])
    for jz in range(nz):
        slot = (z ^ jz) ^ (per * core)
        outs[jz][...] = grads[slot].astype(outs[jz].dtype)


def out_sum_kernel(own_ref, *rest):
    parts, (keep_ref, send_ref) = rest[:-2], rest[-2:]
    total = own_ref[...]
    for part in parts:
        total = total + part[...].astype(F32)
    total = total.astype(BF16)
    keep_ref[...] = total[:BLK]
    send_ref[...] = total[BLK:]


def weight_sum_kernel(own_ref, *rest):
    parts, (keep_ref, send_ref) = rest[:-2], rest[-2:]
    total = own_ref[...]
    for part in parts:
        total = total + part[...].astype(F32)
    half = total.shape[0] // 2
    core = lax.axis_index("seq") % 2
    keep_ref[...] = jnp.where(core == 0, total[:half], total[half:])
    send_ref[...] = jnp.where(core == 0, total[half:], total[:half])


def join_kernel(keep_ref, recv_ref, out_ref):
    core = lax.axis_index("seq") % 2
    half = keep_ref.shape[1]
    lead = (0,) if len(out_ref.shape) == 3 else ()
    keep, recv = keep_ref[...], recv_ref[...]
    out_ref[lead + (slice(None), slice(0, half))] = jnp.where(core == 0, keep, recv)
    out_ref[lead + (slice(None), slice(half, 2 * half))] = jnp.where(core == 0, recv, keep)


def place_kernel(n, per, *rest):
    parts, outs, sems = rest[:n], rest[n : n + 3], rest[n + 3]
    s = lax.axis_index("seq")
    moves = []
    for j in range(n):
        for t in range(3):
            for g in range(per):
                col = col_of(s ^ j, g, n // 2, per)
                moves.append((parts[j].at[t, :, pl.ds(g * HD, HD)], outs[t].at[0, :, pl.ds(col, HD)]))
    copies(moves, sems)


def paired(n, nz, queries, key_rows, values, adjacency, counts, out_weight, out_cotangent):
    per = nz // 2
    length = n * BLK
    wide = queries.shape[2]
    half = wide // 2
    heads = per * HD

    def to(x, j):
        return lax.ppermute(x, "seq", [(i, i ^ j) for i in range(n)])

    def to_z(x, j):
        return lax.ppermute(x, "dp", [(i, i ^ j) for i in range(nz)])

    chunk = sds((3, BLK, heads), BF16)
    piece = sds((BLK, half), BF16)
    prep = call(
        functools.partial(prep_kernel, n, per),
        [(ANY, x) for x in (queries, key_rows, values, out_cotangent, out_weight)],
        [(ANY, chunk)] * n + [(ANY, piece)] * 2 + [(ANY, sds((HD, half), BF16))],
        [pltpu.SemaphoreType.DMA((3 * n * per + 3,))],
        moved=8 * MIB,
    )
    qkv = [prep[0]] + [to(prep[j], j) for j in range(1, n)]
    same, other, wsend = prep[n:]
    wts = [wsend] + [to_z(wsend, j) for j in range(1, nz)]
    cot = [same] + [to(other if j % 2 else same, j) for j in range(1, n)]

    attn, swap, attn_t, lse, bias = call(
        functools.partial(forward_kernel, n, per),
        [(SMEM, adjacency), (SMEM, counts)] + [(VMEM, x) for x in qkv],
        [
            (VMEM, sds((length, heads), BF16)),
            (VMEM, sds((length, heads), BF16)),
            (VMEM, sds((per, HD, length), BF16)),
            (VMEM, sds((per, length), F32)),
            (VMEM, sds((n, length), F32)),
        ],
        [
            pltpu.VMEM((per, length, HD), BF16),
            pltpu.VMEM((per, HD, length), BF16),
            pltpu.VMEM((length, 2 * BLK), F32),
            pltpu.VMEM((length, 2 * BLK), BF16),
        ],
        flops=4 * per * length * length * HD,
        moved=4 * MIB,
    )
    attn_recv = to(swap, 1)

    grad_own, grad_send, w_rows, cot_rows = call(
        functools.partial(grad_attn_kernel, n, per),
        [(VMEM, x) for x in cot + wts],
        [
            (VMEM, sds((heads, length), F32)),
            (VMEM, sds((heads, length), BF16)),
            (VMEM, sds((2 * heads, half), BF16)),
            (VMEM, sds((length, half), BF16)),
        ],
        flops=4 * length * heads * half,
        moved=8 * MIB,
    )
    grad_recv = to(grad_send, 1)

    out_parts = call(
        functools.partial(out_kernel, n),
        [(VMEM, attn), (VMEM, attn_recv), (VMEM, w_rows)],
        [(VMEM, sds((2 * BLK, half), BF16 if t else F32)) for t in range(n // 2)],
        flops=4 * length * heads * half,
        moved=6 * MIB,
    )
    out_recv = [to(out_parts[t], 2 * t) for t in range(1, n // 2)]

    grads = call(
        functools.partial(backward_kernel, n, per),
        [(VMEM, x) for x in qkv + [attn_t, lse, bias, grad_own, grad_recv]],
        [(VMEM, chunk)] * n,
        [
            pltpu.VMEM((per, length, HD), BF16),
            pltpu.VMEM((per, HD, length), BF16),
            pltpu.VMEM((per, HD, length), BF16),
            pltpu.VMEM((per, length), F32),
            pltpu.VMEM((2 * BLK, length), BF16),
            pltpu.VMEM((2 * BLK, length), BF16),
            pltpu.VMEM((HD, length), F32),
        ],
        flops=10 * per * length * length * HD,
        moved=8 * MIB,
    )
    back = [grads[0]] + [to(grads[j], j) for j in range(1, n)]

    w_parts = call(
        functools.partial(weight_kernel, nz),
        [(VMEM, attn_t), (VMEM, attn_recv), (VMEM, cot_rows)],
        [(VMEM, sds((HD, half), BF16 if j else F32)) for j in range(nz)],
        [pltpu.VMEM((nz, HD, half), F32)],
        flops=4 * length * heads * half,
        moved=6 * MIB,
    )
    w_recv = [to_z(w_parts[j], j) for j in range(1, nz)]

    out_keep, out_send = call(
        out_sum_kernel,
        [(VMEM, x) for x in [out_parts[0]] + out_recv],
        [(VMEM, sds((BLK, half), BF16))] * 2,
        moved=3 * MIB,
    )
    (layer_out,) = call(
        join_kernel,
        [(VMEM, out_keep), (VMEM, to(out_send, 1))],
        [(VMEM, sds((1, BLK, wide), BF16))],
        moved=MIB,
    )
    w_keep, w_send = call(
        weight_sum_kernel,
        [(VMEM, x) for x in [w_parts[0]] + w_recv],
        [(VMEM, sds((HD // 2, half), F32))] * 2,
        moved=2 * MIB,
    )
    (weight_grad,) = call(
        join_kernel,
        [(VMEM, w_keep), (VMEM, to(w_send, 1))],
        [(VMEM, sds((HD // 2, wide), F32))],
        moved=MIB,
    )
    token = sds((1, BLK, wide), BF16)
    query_grad, key_grad, value_grad = call(
        functools.partial(place_kernel, n, per),
        [(ANY, x) for x in back],
        [(ANY, token)] * 3,
        [pltpu.SemaphoreType.DMA((3 * n * per,))],
        moved=3 * MIB,
    )
    return layer_out, query_grad, key_grad, value_grad, weight_grad


def solution(mesh):
    in_specs = (
        P("dp", "seq", None),
        P("dp", "seq", None),
        P("dp", "seq", None),
        P("dp", None, None),
        P("dp", None),
        P("dp", None),
        P("dp", "seq", None),
    )
    out_specs = (
        P("dp", "seq", None),
        P("dp", "seq", None),
        P("dp", "seq", None),
        P("dp", "seq", None),
        P(("dp", "seq"), None),
    )
    n, nz = mesh.shape["seq"], mesh.shape["dp"]

    def body(queries, *rest):
        heads = queries.shape[2] // HD
        fits = queries.shape[1] == BLK and heads == nz * (n // 2)
        if fits and n % 2 == 0 and nz % 2 == 0 and n & (n - 1) == 0 and nz & (nz - 1) == 0:
            return paired(n, nz, queries, *rest)
        return local(queries, *rest)

    return jax.shard_map(body, mesh=mesh, in_specs=in_specs, out_specs=out_specs, check_vma=False)
```

```python
import functools

import jax
import jax.numpy as jnp
from jax import lax
from jax.experimental import pallas as pl
from jax.experimental.pallas import tpu as pltpu
from jax.sharding import PartitionSpec as P

HD = 128
BLK = 128
NBR = 8
F32 = jnp.float32
BF16 = jnp.bfloat16
NN = (((1,), (0,)), ((), ()))
NT = (((1,), (1,)), ((), ()))
LOG2E = 1.4426950408889634
DEAD = -1e30
VMEM = pl.BlockSpec(memory_space=pltpu.VMEM)
SMEM = pl.BlockSpec(memory_space=pltpu.SMEM)
HBM = pl.BlockSpec(memory_space=pltpu.HBM)
ANY = pl.BlockSpec(memory_space=pl.ANY)
MIB = 1 << 20


def mm(a, b, dims=NN):
    return lax.dot_general(a, b, dims, preferred_element_type=F32)


def in_hbm(x):
    return pltpu.with_memory_space_constraint(x, pltpu.HBM)


def sds(shape, dtype):
    return jax.ShapeDtypeStruct(shape, dtype)


def after(x, *deps):
    return lax.optimization_barrier((x,) + deps)[0]


def call(kernel, ins, outs, scratch=(), flops=0, moved=0, vmem=24):
    return pl.pallas_call(
        kernel,
        out_shape=tuple(shape for _, shape in outs),
        in_specs=[spec for spec, _ in ins],
        out_specs=tuple(spec for spec, _ in outs),
        scratch_shapes=list(scratch),
        compiler_params=pltpu.CompilerParams(vmem_limit_bytes=vmem * MIB),
        cost_estimate=pl.CostEstimate(flops=flops, bytes_accessed=moved, transcendentals=0),
    )(*[arg for _, arg in ins])


def col_of(dev, g, pairs, per):
    return pl.multiple_of(((dev % 2 * per + g) * pairs + dev // 2) * HD, HD)


def copies(moves, sems):
    handles = [pltpu.make_async_copy(src, dst, sems.at[n]) for n, (src, dst) in enumerate(moves)]
    for handle in handles:
        handle.start()
    for handle in handles:
        handle.wait()


def attend(query_blk, key_blk, value_blk, links, live_count):
    scale = HD ** (-0.5)
    blocks = query_blk.shape[0]
    heads = query_blk.shape[2]
    key_near = key_blk[links].reshape(blocks, NBR * BLK, heads, HD)
    value_near = value_blk[links].reshape(blocks, NBR * BLK, heads, HD)
    scores = (
        jnp.einsum("iqhd,ikhd->hiqk", query_blk, key_near, preferred_element_type=jnp.float32)
        * scale
    )
    live = (jnp.arange(NBR * BLK) // BLK)[None, :] < live_count[:, None]
    scores = jnp.where(live[None, :, None, :], scores, -1e30)
    highest = jnp.max(scores, axis=-1, keepdims=True)
    expo = jnp.exp(scores - highest)
    prob = expo / jnp.sum(expo, axis=-1, keepdims=True)
    prob_bf = prob.astype(jnp.bfloat16)
    attended = jnp.einsum(
        "hiqk,ikhd->iqhd", prob_bf, value_near, preferred_element_type=jnp.float32
    ).astype(jnp.bfloat16)
    return (prob, prob_bf, attended, key_near, value_near)


def backward(query_blk, links, grad_blk, prob, prob_bf, attended, key_near, value_near):
    scale = HD ** (-0.5)
    blocks = query_blk.shape[0]
    heads = query_blk.shape[2]
    value_part = jnp.einsum(
        "hiqk,iqhd->ikhd", prob_bf, grad_blk, preferred_element_type=jnp.float32
    )
    grad_prob = jnp.einsum(
        "iqhd,ikhd->hiqk", grad_blk, value_near, preferred_element_type=jnp.float32
    )
    delta = jnp.einsum("iqhd,iqhd->hiq", grad_blk, attended, preferred_element_type=jnp.float32)
    score_grad = (prob * (grad_prob - delta[..., None]) * scale).astype(jnp.bfloat16)
    query_grad = jnp.einsum(
        "hiqk,ikhd->iqhd", score_grad, key_near, preferred_element_type=jnp.float32
    ).astype(jnp.bfloat16)
    key_part = jnp.einsum(
        "hiqk,iqhd->ikhd", score_grad, query_blk, preferred_element_type=jnp.float32
    )
    member = (links.reshape(-1)[None, :] == jnp.arange(blocks)[:, None]).astype(jnp.float32)
    key_grad = jnp.einsum(
        "ja,aqhd->jqhd",
        member,
        key_part.reshape(blocks * NBR, BLK, heads, HD),
        precision=lax.Precision.HIGHEST,
    )
    value_grad = jnp.einsum(
        "ja,aqhd->jqhd",
        member,
        value_part.reshape(blocks * NBR, BLK, heads, HD),
        precision=lax.Precision.HIGHEST,
    )
    return (query_grad, key_grad.astype(jnp.bfloat16), value_grad.astype(jnp.bfloat16))


def local(queries, key_rows, values, adjacency, counts, out_weight, out_cotangent):
    query_heads, key_heads, value_heads = (
        lax.all_to_all(queries[0], "seq", split_axis=1, concat_axis=0, tiled=True),
        lax.all_to_all(key_rows[0], "seq", split_axis=1, concat_axis=0, tiled=True),
        lax.all_to_all(values[0], "seq", split_axis=1, concat_axis=0, tiled=True),
    )
    length = query_heads.shape[0]
    blocks = length // BLK
    heads = query_heads.shape[1] // HD
    shape = (blocks, BLK, heads, HD)
    links = adjacency[0]
    live_count = counts[0]
    query_blk = query_heads.reshape(shape)
    prob, prob_bf, attended, key_near, value_near = attend(
        query_blk, key_heads.reshape(shape), value_heads.reshape(shape), links, live_count
    )
    attn_tokens = lax.all_to_all(
        attended.reshape(length, heads * HD), "seq", split_axis=0, concat_axis=1, tiled=True
    )
    cotangent = out_cotangent[0]
    columns = attn_tokens
    layer_out = jnp.dot(
        columns,
        lax.all_gather(out_weight, "dp", axis=0, tiled=True),
        preferred_element_type=jnp.float32,
    )
    grad_tokens = lax.dot_general(
        cotangent,
        lax.all_gather(out_weight, "dp", axis=0, tiled=True),
        (((1,), (1,)), ((), ())),
        preferred_element_type=jnp.float32,
    )
    grad_heads = lax.all_to_all(
        grad_tokens.astype(jnp.bfloat16), "seq", split_axis=1, concat_axis=0, tiled=True
    )
    query_grad, key_grad, value_grad = backward(
        query_blk, links, grad_heads.reshape(shape), prob, prob_bf, attended, key_near, value_near
    )
    query_back, key_back, value_back = (
        lax.all_to_all(
            query_grad.reshape(length, heads * HD), "seq", split_axis=0, concat_axis=1, tiled=True
        ),
        lax.all_to_all(
            key_grad.reshape(length, heads * HD), "seq", split_axis=0, concat_axis=1, tiled=True
        ),
        lax.all_to_all(
            value_grad.reshape(length, heads * HD), "seq", split_axis=0, concat_axis=1, tiled=True
        ),
    )
    columns = attn_tokens
    weight_grad = lax.psum_scatter(
        lax.dot_general(
            columns, cotangent, (((0,), (0,)), ((), ())), preferred_element_type=jnp.float32
        ),
        ("dp", "seq"),
        scatter_dimension=0,
        tiled=True,
    )
    return (
        layer_out.astype(jnp.bfloat16)[None],
        query_back[None],
        key_back[None],
        value_back[None],
        weight_grad,
    )


def prep_kernel(n, per, q_ref, k_ref, v_ref, c_ref, *rest):
    qkv, (same, other, sems) = by_slot(rest[:-3], n, OPT["q_order"]), rest[-3:]
    s = lax.axis_index("seq")
    core = s % 2
    half = c_ref.shape[2] // 2
    moves = []
    for j in range(n):
        for t, src in enumerate((q_ref, k_ref, v_ref)):
            for g in range(per):
                col = col_of(s ^ j, g, n // 2, per)
                moves.append((src.at[0, :, pl.ds(col, HD)], qkv[j].at[t, :, pl.ds(g * HD, HD)]))
    mine = pl.multiple_of(core * half, half)
    theirs = pl.multiple_of((1 - core) * half, half)
    moves.append((c_ref.at[0, :, pl.ds(mine, half)], same))
    moves.append((c_ref.at[0, :, pl.ds(theirs, half)], other))
    copies(moves, sems)


def rows_prep_kernel(w_ref, out_ref, sem):
    s = lax.axis_index("seq")
    half = out_ref.shape[1]
    row = pl.multiple_of((s // 2) * HD, HD)
    col = pl.multiple_of((s % 2) * half, half)
    copy = pltpu.make_async_copy(w_ref.at[pl.ds(row, HD), pl.ds(col, half)], out_ref, sem)
    copy.start()
    copy.wait()


def by_slot(refs, n, order):
    if len(refs) == n:
        slots = dict(zip([0] + order, refs))
        return [slots[j] for j in range(n)]
    if len(refs) == 2:
        return [refs[j % 2].at[j // 2] for j in range(n)]
    return [refs[j // 2].at[j % 2] for j in range(n)]


def merge_kernel(mine_ref, recv_ref, *outs):
    for jc, out in enumerate(outs):
        out[0] = mine_ref[jc]
        out[1] = recv_ref[jc]


def stack_kernel(first_ref, second_ref, out_ref):
    rows = first_ref.shape[0]
    out_ref[:rows] = first_ref[...]
    out_ref[rows:] = second_ref[...]


def forward_kernel(n, per, adj_ref, cnt_ref, *rest):
    qkv, rest = by_slot(rest[:-9], n, OPT["q_order"]), rest[-9:]
    attn_ref, swap_ref, attn_t_ref, lse_ref, bias_ref, keys, vals_t, score, expo = rest
    s = lax.axis_index("seq")
    length = n * BLK
    scale = HD**-0.5 * LOG2E
    place = lax.broadcasted_iota(jnp.int32, (n, BLK), 0)
    for i in range(n):
        block = s ^ i
        count = cnt_ref[0, block]
        bias = jnp.full((n, BLK), DEAD, F32)
        for slot in range(NBR):
            j = jnp.where(slot < count, adj_ref[0, block, slot] ^ s, n)
            bias = jnp.where(place == j, 0.0, bias)
        bias_ref[:, i * BLK : (i + 1) * BLK] = bias
    tile = 2 * BLK
    for g in range(per):
        lanes = slice(g * HD, (g + 1) * HD)
        for j in range(n):
            rows = slice(j * BLK, (j + 1) * BLK)
            keys[g, rows, :] = qkv[j][1, :, lanes]
            vals_t[g, :, rows] = qkv[j][2, :, lanes].T
        for t in range(length // tile):
            cols = slice(t * tile, (t + 1) * tile)
            query = jnp.concatenate([qkv[2 * t][0, :, lanes], qkv[2 * t + 1][0, :, lanes]], axis=0)
            highest = jnp.full((1, tile), -jnp.inf, F32)
            for j in range(n):
                rows = slice(j * BLK, (j + 1) * BLK)
                part = mm(keys[g, rows, :], query, NT) * scale + bias_ref[j : j + 1, cols]
                score[rows, :] = part
                highest = jnp.maximum(highest, jnp.max(part, axis=0, keepdims=True))
            total = jnp.zeros((1, tile), F32)
            for j in range(n):
                rows = slice(j * BLK, (j + 1) * BLK)
                part = jnp.exp2(score[rows, :] - highest)
                total = total + jnp.sum(part, axis=0, keepdims=True)
                expo[rows, :] = part.astype(BF16)
            att = (mm(vals_t[g], expo[...]) * (1.0 / total)).astype(BF16)
            attn_t_ref[g, :, cols] = att
            lse_ref[g : g + 1, cols] = highest + jnp.log2(total)
            first, second = att[:, :BLK].T, att[:, BLK:].T
            base = t * tile
            attn_ref[base : base + BLK, lanes] = first
            attn_ref[base + BLK : base + tile, lanes] = second
            swap_ref[base : base + BLK, lanes] = second
            swap_ref[base + BLK : base + tile, lanes] = first


def grow_kernel(bit, mine_ref, recv_ref, out_ref):
    here = lax.axis_index("dp") // bit % 2
    for i in range(mine_ref.shape[0]):
        out_ref[2 * i + here] = mine_ref[i]
        out_ref[2 * i + 1 - here] = recv_ref[i]


def halve(total, bit, keep_ref, send_ref):
    here = lax.axis_index("dp") // bit % 2
    for i in range(keep_ref.shape[0]):
        keep_ref[i] = jnp.where(here == 0, total[2 * i], total[2 * i + 1])
        send_ref[i] = jnp.where(here == 0, total[2 * i + 1], total[2 * i]).astype(BF16)


def fold_kernel(bit, mine_ref, recv_ref, keep_ref, send_ref):
    halve(mine_ref[...] + recv_ref[...].astype(F32), bit, keep_ref, send_ref)


def rows_kernel(*refs):
    z = lax.axis_index("dp")
    for j, ref in enumerate(refs[:-1]):
        refs[-1][z ^ j] = ref[0]


def grad_attn_kernel(n, per, *rest):
    cot, rest = rest[:-4], rest[-4:]
    w_ref, own_ref, send_ref, cot_out = rest
    core = lax.axis_index("seq") % 2
    mine = w_ref[pl.ds(pl.multiple_of(core * per * HD, HD), per * HD), :]
    theirs = w_ref[pl.ds(pl.multiple_of((1 - core) * per * HD, HD), per * HD), :]
    rows = n * BLK // len(cot)
    for j, ref in enumerate(cot):
        cot_out[j * rows : (j + 1) * rows, :] = ref[...]
    for t in range(n // 2):
        base = 2 * t * BLK
        rows = cot_out[base : base + 2 * BLK, :]
        own_ref[:, base : base + 2 * BLK] = mm(mine, rows, NT)
        part = mm(theirs, rows, NT).astype(BF16)
        send_ref[:, base : base + BLK] = part[:, BLK:]
        send_ref[:, base + BLK : base + 2 * BLK] = part[:, :BLK]


def backward_kernel(n, per, n_outs, *rest):
    queries, keys_t, grad, delta, probs, dscores, dq_t = rest[-7:]
    qkv = by_slot(rest[: -12 - n_outs], n, OPT["q_order"])
    outs = by_slot(rest[-7 - n_outs : -7], n, OPT["g_order"])
    attn_t_ref, lse_ref, bias_ref, own_ref, recv_ref = rest[-12 - n_outs : -7 - n_outs]
    scale = HD**-0.5
    tile = 2 * BLK
    length = n * BLK
    for g in range(per):
        lanes = slice(g * HD, (g + 1) * HD)
        grad_t = (own_ref[lanes, :] + recv_ref[lanes, :].astype(F32)).astype(BF16)
        grad[g] = grad_t
        delta[g : g + 1, :] = jnp.sum(
            grad_t.astype(F32) * attn_t_ref[g].astype(F32), axis=0, keepdims=True
        )
        for j in range(n):
            rows = slice(j * BLK, (j + 1) * BLK)
            queries[g, rows, :] = qkv[j][0, :, lanes]
            keys_t[g, :, rows] = qkv[j][1, :, lanes].T
        for t in range(length // tile):
            key = jnp.concatenate([qkv[2 * t][1, :, lanes], qkv[2 * t + 1][1, :, lanes]], axis=0)
            value = jnp.concatenate([qkv[2 * t][2, :, lanes], qkv[2 * t + 1][2, :, lanes]], axis=0)
            for u in range(length // tile):
                cols = slice(u * tile, (u + 1) * tile)
                score = mm(key, queries[g, cols, :], NT)
                dprob = mm(value, grad[g, :, cols])
                lse = lse_ref[g : g + 1, cols]
                dlt = delta[g : g + 1, cols]
                for b in range(2):
                    rows = slice(b * BLK, (b + 1) * BLK)
                    shift = bias_ref[2 * t + b : 2 * t + b + 1, cols] - lse
                    prob = jnp.exp2(score[rows] * (scale * LOG2E) + shift)
                    probs[rows, cols] = prob.astype(BF16)
                    dscores[rows, cols] = (prob * (dprob[rows] - dlt)).astype(BF16)
            dvalue = mm(probs[...], grad[g], NT).astype(BF16)
            dkey = (mm(dscores[...], queries[g]) * scale).astype(BF16)
            for b in range(2):
                rows = slice(b * BLK, (b + 1) * BLK)
                outs[2 * t + b][1, :, lanes] = dkey[rows]
                outs[2 * t + b][2, :, lanes] = dvalue[rows]
            part = mm(keys_t[g, :, t * tile : (t + 1) * tile], dscores[...])
            if t == 0:
                dq_t[...] = part
            else:
                dq_t[...] += part
        for j in range(n):
            rows = slice(j * BLK, (j + 1) * BLK)
            outs[j][0, :, lanes] = (dq_t[:, rows].T * scale).astype(BF16)


def out_kernel(n, attn_ref, recv_ref, w_ref, *outs):
    core = lax.axis_index("seq") % 2
    tile = 2 * BLK
    heads = attn_ref.shape[1]
    mine = w_ref[pl.ds(pl.multiple_of(core * heads, heads), heads), :]
    theirs = w_ref[pl.ds(pl.multiple_of((1 - core) * heads, heads), heads), :]
    for t in range(n // 2):
        rows = slice(t * tile, (t + 1) * tile)
        part = mm(attn_ref[rows, :], mine) + mm(recv_ref[rows, :], theirs)
        if len(outs) > n // 2 and t == 3:
            outs[3][...] = part[:BLK].astype(BF16)
            outs[4][...] = part[BLK:].astype(BF16)
        else:
            outs[t][...] = part.astype(outs[t].dtype)


def relay_kernel(first_ref, first_recv, second_ref, second_recv, *outs):
    outs[0][:BLK] = first_ref[:BLK]
    outs[0][BLK:] = (first_ref[BLK:].astype(F32) + second_recv[...].astype(F32)).astype(BF16)
    outs[1][:BLK] = (second_ref[:BLK].astype(F32) + first_recv[...].astype(F32)).astype(BF16)
    outs[1][BLK:] = second_ref[BLK:]


def weight_kernel(per, attn_t_ref, recv_ref, cot_ref, *rest):
    outs, grads = rest[:-1], rest[-1]
    core = lax.axis_index("seq") % 2
    for g in range(per):
        grads[core * per + g] = mm(attn_t_ref[g], cot_ref[...])
        recv = recv_ref[:, g * HD : (g + 1) * HD].T
        grads[(1 - core) * per + g] = mm(recv, cot_ref[...])
    if len(outs) == 2:
        halve(grads, 1, *outs)
    else:
        z = lax.axis_index("dp")
        for j, out in enumerate(outs):
            out[0] = grads[z ^ j].astype(out.dtype)


def out_sum_kernel(own_ref, *rest):
    parts, (keep_ref, send_ref) = rest[:-2], rest[-2:]
    total = own_ref[...]
    for part in parts:
        total = total + part[...].astype(F32)
    total = total.astype(BF16)
    keep_ref[...] = total[:BLK]
    send_ref[...] = total[BLK:]


def weight_sum_kernel(own_ref, *rest):
    parts, (keep_ref, send_ref) = rest[:-2], rest[-2:]
    total = own_ref[0]
    for part in parts:
        total = total + part[0].astype(F32)
    half = total.shape[0] // 2
    core = lax.axis_index("seq") % 2
    keep_ref[...] = jnp.where(core == 0, total[:half], total[half:])
    send_ref[...] = jnp.where(core == 0, total[half:], total[:half])


def join_kernel(keep_ref, recv_ref, out_ref):
    core = lax.axis_index("seq") % 2
    half = keep_ref.shape[1]
    lead = (0,) if len(out_ref.shape) == 3 else ()
    keep, recv = keep_ref[...].astype(out_ref.dtype), recv_ref[...].astype(out_ref.dtype)
    out_ref[lead + (slice(None), slice(0, half))] = jnp.where(core == 0, keep, recv)
    out_ref[lead + (slice(None), slice(half, 2 * half))] = jnp.where(core == 0, recv, keep)


def place_kernel(n, per, *rest):
    parts, outs, sems = by_slot(rest[:-4], n, OPT["g_order"]), rest[-4:-1], rest[-1]
    s = lax.axis_index("seq")
    moves = []
    for j in range(n):
        for t in range(3):
            for g in range(per):
                col = col_of(s ^ j, g, n // 2, per)
                moves.append((parts[j].at[t, :, pl.ds(g * HD, HD)], outs[t].at[0, :, pl.ds(col, HD)]))
    copies(moves, sems)


OPT = {'q_order': [6, 2, 4, 7, 3, 5, 1], 'g_order': [6, 2, 4, 7, 3, 5, 1], 'c_order': [1, 2, 3], 'tie_swap': [], 'q_merged': False, 'g_merged': False, 'c_gather': False, 'w_hyper': True, 'g_hyper': True, 'out_first': False, 'wgt_first': True, 'g_tied': False, 'o_order': [3, 2, 1], 'tie_other': [], 'tie_cot': ['q6', 'q2', 'q4'], 'tie_wsend': [], 'tie_w_last': [], 'tie_k1': [], 'tie_out': ['k2'], 'tie_k2': [], 'tie_wgt': [], 'tie_k3': ['wgt'], 'tie_fold': ['k3'], 'tie_osum': ['k3'], 'o_fwd': True, 'tie_relay': [], 'tie_place': [], 'relay_first': False, 'tie_prep': []}


def paired(n, nz, queries, key_rows, values, adjacency, counts, out_weight, out_cotangent):
    per = nz // 2
    pairs = n // 2
    length = n * BLK
    wide = queries.shape[2]
    half = wide // 2
    heads = per * HD
    chunk = sds((3, BLK, heads), BF16)
    couple = sds((2, 3, BLK, heads), BF16)
    chunks = sds((pairs, 3, BLK, heads), BF16)
    piece = sds((BLK, half), BF16)
    named = {}

    def tied(x, point):
        deps = [named[d] for d in OPT["tie_" + point]]
        return after(x, *deps) if deps else x

    def to(x, j):
        return lax.ppermute(x, "seq", [(i, i ^ j) for i in range(n)])

    def to_z(x, j):
        return lax.ppermute(x, "dp", [(i, i ^ j) for i in range(nz)])

    def exchange(parts, name, merged, ties=None):
        if merged:
            parts = call(
                merge_kernel,
                [(VMEM, parts[0]), (VMEM, to(parts[1], 1))],
                [(VMEM, couple)] * pairs,
                moved=4 * MIB,
            )
            out = [parts[0]]
            for jc in range(1, pairs):
                x = after(parts[jc], ties[jc]) if ties else parts[jc]
                out.append(to(x, 2 * jc))
                named[name + str(2 * jc)] = out[-1]
            named[name + "1"] = named[name + "7"] = out[1]
            return out
        out = [parts[0]]
        for part, j in zip(parts[1:], OPT[name + "_order"]):
            x = after(part, ties[j // 2]) if ties and j > 1 else part
            out.append(to(x, j))
            named[name + str(j)] = out[-1]
        return out

    lay = [chunks] * 2 if OPT["q_merged"] else [chunk] * n
    (wsend,) = call(
        rows_prep_kernel,
        [(HBM, in_hbm(out_weight))],
        [(VMEM, pltpu.VMEM((HD, half), BF16))],
        [pltpu.SemaphoreType.DMA],
    )
    named["ws"] = wsend
    prep = call(
        functools.partial(prep_kernel, n, per),
        [(HBM, in_hbm(x)) for x in (tied(queries, "prep"), key_rows, values, out_cotangent)],
        [(VMEM, pltpu.VMEM(x.shape, x.dtype)) for x in lay + [piece] * 2],
        [pltpu.SemaphoreType.DMA((3 * n * per + 2,))],
        moved=8 * MIB,
    )
    same, other = prep[-2:]
    named["same"] = same
    qkv = exchange(prep[:-2], "q", OPT["q_merged"])
    if OPT["c_gather"] == 2:
        same, other = tied(same, "cot"), tied(other, "cot")
        cot = [same] + [to(other if j % 2 else same, j) for j in range(1, n)]
        named["c0"] = cot[1]
    elif OPT["c_gather"]:
        same = tied(same, "cot")
        cot = [same, to(tied(other, "other"), 1)] + [None] * (n - 2)
        for j in sorted(range(2, n), key=lambda j: ((j >> 1).bit_count(), j & 1, j)):
            bits = j & ~1
            hop = bits & -bits if j % 2 == 0 else 1 << (bits.bit_length() - 1)
            cot[j] = to(cot[j ^ hop], hop)
        named["c0"] = cot[1]
    else:
        (cot_own,) = call(
            stack_kernel,
            [(VMEM, same), (VMEM, to(tied(other, "other"), 1))],
            [(VMEM, sds((2 * BLK, half), BF16))],
            moved=MIB,
        )
        named["c0"] = cot_own
        cot_sent = tied(cot_own, "cot")
        cot = [cot_own, None, None, None]
        for jc in OPT["c_order"]:
            cot[jc] = to(cot_sent, 2 * jc)
            named["c" + str(jc)] = cot[jc]
    w_rows = tied(wsend, "wsend")[None]
    if OPT["w_hyper"]:
        bit = nz
        while bit > 1:
            bit //= 2
            (w_rows,) = call(
                functools.partial(grow_kernel, bit),
                [(VMEM, w_rows), (VMEM, to_z(w_rows, bit))],
                [(VMEM, sds((2 * w_rows.shape[0], HD, half), BF16))],
                moved=2 * MIB,
            )
            named.setdefault("w1", w_rows)
    else:
        named["w1"] = to_z(w_rows, 2)
        wts = [w_rows, None, named["w1"]] + [to_z(w_rows, j) for j in range(3, nz)]
        wts[1] = to_z(tied(w_rows, "w_last"), 1)
        (w_rows,) = call(
            rows_kernel,
            [(VMEM, x) for x in wts],
            [(VMEM, sds((nz, HD, half), BF16))],
            moved=2 * MIB,
        )
    w_rows = w_rows.reshape(nz * HD, half)
    named["w"] = w_rows

    attn, swap, attn_t, lse, bias = call(
        functools.partial(forward_kernel, n, per),
        [(SMEM, adjacency), (SMEM, tied(counts, "k1"))] + [(VMEM, x) for x in qkv],
        [
            (VMEM, sds((length, heads), BF16)),
            (VMEM, sds((length, heads), BF16)),
            (VMEM, sds((per, HD, length), BF16)),
            (VMEM, sds((per, length), F32)),
            (VMEM, sds((n, length), F32)),
        ],
        [
            pltpu.VMEM((per, length, HD), BF16),
            pltpu.VMEM((per, HD, length), BF16),
            pltpu.VMEM((length, 2 * BLK), F32),
            pltpu.VMEM((length, 2 * BLK), BF16),
        ],
        flops=4 * per * length * length * HD,
        moved=4 * MIB,
    )
    attn_recv = to(tied(swap, "swap"), 1)
    named["a"] = attn_recv

    def project():
        shapes = [sds((2 * BLK, half), BF16 if t else F32) for t in range(pairs)]
        if OPT["o_fwd"]:
            shapes = shapes[:3] + [sds((BLK, half), BF16)] * 2
        parts = call(
            functools.partial(out_kernel, n),
            [(VMEM, attn), (VMEM, attn_recv), (VMEM, tied(w_rows, "out"))],
            [(VMEM, x) for x in shapes],
            flops=4 * length * heads * half,
            moved=6 * MIB,
        )
        named["o0"] = parts[0]
        if OPT["o_fwd"]:
            named["o1"] = to(parts[3], 2)
            named["o2"] = to(parts[4], 4)
            return parts, [named["o1"], named["o2"]]
        recv = [None] * pairs
        for t in OPT["o_order"]:
            recv[t] = to(parts[t], 2 * t)
            named["o" + str(t)] = recv[t]
        return parts, recv[1:]

    if OPT["out_first"]:
        out_parts, out_recv = project()
    grad_own, grad_send, cot_rows = call(
        functools.partial(grad_attn_kernel, n, per),
        [(VMEM, x) for x in cot + [tied(w_rows, "k2")]],
        [
            (VMEM, sds((heads, length), F32)),
            (VMEM, sds((heads, length), BF16)),
            (VMEM, sds((length, half), BF16)),
        ],
        flops=4 * length * heads * half,
        moved=8 * MIB,
    )
    named["k2"] = grad_own
    grad_recv = to(grad_send, 1)
    if not OPT["out_first"]:
        out_parts, out_recv = project()

    def weigh():
        outs = [(2, F32), (2, BF16)] if OPT["g_hyper"] else [(1, F32)] + [(1, BF16)] * (nz - 1)
        return call(
            functools.partial(weight_kernel, per),
            [(VMEM, attn_t), (VMEM, attn_recv), (VMEM, tied(cot_rows, "wgt"))],
            [(VMEM, sds((m, HD, half), d)) for m, d in outs],
            [pltpu.VMEM((nz, HD, half), F32)],
            flops=4 * length * heads * half,
            moved=6 * MIB,
        )

    def relay(first, second):
        relayed = call(
            relay_kernel,
            [(VMEM, tied(out_parts[1], "relay")), (VMEM, first), (VMEM, out_parts[2]), (VMEM, second)],
            [(VMEM, sds((2 * BLK, half), BF16))] * 2,
            moved=3 * MIB,
        )
        named["r"] = relayed[0]
        recv = [to(relayed[0], 2), to(relayed[1], 4)]
        named["o3"] = recv[0]
        return recv

    if OPT["o_fwd"] and OPT["relay_first"]:
        out_recv = relay(*out_recv)
    if OPT["wgt_first"]:
        weighed = weigh()
        named["wgt"] = weighed[0]
    lay = [chunks] * 2 if OPT["g_merged"] else [chunk] * n
    grads = call(
        functools.partial(backward_kernel, n, per, len(lay)),
        [(VMEM, x) for x in qkv + [attn_t, lse, bias, tied(grad_own, "k3"), grad_recv]],
        [(VMEM, x) for x in lay],
        [
            pltpu.VMEM((per, length, HD), BF16),
            pltpu.VMEM((per, HD, length), BF16),
            pltpu.VMEM((per, HD, length), BF16),
            pltpu.VMEM((per, length), F32),
            pltpu.VMEM((2 * BLK, length), BF16),
            pltpu.VMEM((2 * BLK, length), BF16),
            pltpu.VMEM((HD, length), F32),
        ],
        flops=10 * per * length * length * HD,
        moved=8 * MIB,
    )
    named["k3"] = grads[0]
    if OPT["o_fwd"] and not OPT["relay_first"]:
        out_recv = relay(*out_recv)
    back = exchange(grads, "g", OPT["g_merged"], [None] + out_recv if OPT["g_tied"] and not OPT["o_fwd"] else None)
    if not OPT["wgt_first"]:
        weighed = weigh()

    if OPT["g_hyper"]:
        w_keep, w_send = weighed
        bit = 1
        while 2 * bit < nz:
            w_keep, w_send = call(
                functools.partial(fold_kernel, 2 * bit),
                [(VMEM, tied(w_keep, "fold")), (VMEM, to_z(w_send, bit))],
                [(VMEM, sds((w_keep.shape[0] // 2, HD, half), d)) for d in (F32, BF16)],
                moved=2 * MIB,
            )
            bit *= 2
        w_all = [w_keep, to_z(w_send, bit)]
    else:
        w_all = [weighed[0]] + [to_z(x, j) for j, x in enumerate(weighed[1:], 1)]

    out_keep, out_send = call(
        out_sum_kernel,
        [(VMEM, x) for x in [tied(out_parts[0], "osum")] + out_recv],
        [(VMEM, sds((BLK, half), BF16))] * 2,
        moved=3 * MIB,
    )
    (layer_out,) = call(
        join_kernel,
        [(VMEM, out_keep), (VMEM, to(out_send, 1))],
        [(VMEM, sds((1, BLK, wide), BF16))],
        moved=MIB,
    )
    half_keep, half_send = call(
        weight_sum_kernel,
        [(VMEM, x) for x in w_all],
        [(VMEM, sds((HD // 2, half), F32))] * 2,
        moved=2 * MIB,
    )
    (weight_grad,) = call(
        join_kernel,
        [(VMEM, half_keep), (VMEM, to(half_send, 1))],
        [(VMEM, sds((HD // 2, wide), F32))],
        moved=MIB,
    )
    named["lo"], named["wg"] = layer_out, weight_grad
    token = sds((1, BLK, wide), BF16)
    query_grad, key_grad, value_grad = call(
        functools.partial(place_kernel, n, per),
        [(ANY, tied(back[0], "place"))] + [(ANY, x) for x in back[1:]],
        [(ANY, token)] * 3,
        [pltpu.SemaphoreType.DMA((3 * n * per,))],
        moved=3 * MIB,
    )
    return layer_out, query_grad, key_grad, value_grad, weight_grad


def solution(mesh):
    in_specs = (
        P("dp", "seq", None),
        P("dp", "seq", None),
        P("dp", "seq", None),
        P("dp", None, None),
        P("dp", None),
        P("dp", None),
        P("dp", "seq", None),
    )
    out_specs = (
        P("dp", "seq", None),
        P("dp", "seq", None),
        P("dp", "seq", None),
        P("dp", "seq", None),
        P(("dp", "seq"), None),
    )
    n, nz = mesh.shape["seq"], mesh.shape["dp"]

    def body(queries, *rest):
        heads = queries.shape[2] // HD
        fits = queries.shape[1] == BLK and heads == nz * (n // 2)
        if fits and n % 2 == 0 and nz % 2 == 0 and n & (n - 1) == 0 and nz & (nz - 1) == 0:
            return paired(n, nz, queries, *rest)
        return local(queries, *rest)

    return jax.shard_map(body, mesh=mesh, in_specs=in_specs, out_specs=out_specs, check_vma=False)
```

```python
import functools

import jax
import jax.numpy as jnp
from jax import lax
from jax.experimental import pallas as pl
from jax.experimental.pallas import tpu as pltpu
from jax.sharding import PartitionSpec as P

HD = 128
BLK = 128
NBR = 8
F32 = jnp.float32
BF16 = jnp.bfloat16
NN = (((1,), (0,)), ((), ()))
NT = (((1,), (1,)), ((), ()))
LOG2E = 1.4426950408889634
DEAD = -1e30
VMEM = pl.BlockSpec(memory_space=pltpu.VMEM)
SMEM = pl.BlockSpec(memory_space=pltpu.SMEM)
HBM = pl.BlockSpec(memory_space=pltpu.HBM)
ANY = pl.BlockSpec(memory_space=pl.ANY)
MIB = 1 << 20


def mm(a, b, dims=NN):
    return lax.dot_general(a, b, dims, preferred_element_type=F32)


def in_hbm(x):
    return pltpu.with_memory_space_constraint(x, pltpu.HBM)


def sds(shape, dtype):
    return jax.ShapeDtypeStruct(shape, dtype)


def after(x, *deps):
    return lax.optimization_barrier((x,) + deps)[0]


def call(kernel, ins, outs, scratch=(), flops=0, moved=0, vmem=24):
    return pl.pallas_call(
        kernel,
        out_shape=tuple(shape for _, shape in outs),
        in_specs=[spec for spec, _ in ins],
        out_specs=tuple(spec for spec, _ in outs),
        scratch_shapes=list(scratch),
        compiler_params=pltpu.CompilerParams(vmem_limit_bytes=vmem * MIB),
        cost_estimate=pl.CostEstimate(flops=flops, bytes_accessed=moved, transcendentals=0),
    )(*[arg for _, arg in ins])


def col_of(dev, g, pairs, per):
    return pl.multiple_of(((dev % 2 * per + g) * pairs + dev // 2) * HD, HD)


def copies(moves, sems):
    handles = [pltpu.make_async_copy(src, dst, sems.at[n]) for n, (src, dst) in enumerate(moves)]
    for handle in handles:
        handle.start()
    for handle in handles:
        handle.wait()


def attend(query_blk, key_blk, value_blk, links, live_count):
    scale = HD ** (-0.5)
    blocks = query_blk.shape[0]
    heads = query_blk.shape[2]
    key_near = key_blk[links].reshape(blocks, NBR * BLK, heads, HD)
    value_near = value_blk[links].reshape(blocks, NBR * BLK, heads, HD)
    scores = (
        jnp.einsum("iqhd,ikhd->hiqk", query_blk, key_near, preferred_element_type=jnp.float32)
        * scale
    )
    live = (jnp.arange(NBR * BLK) // BLK)[None, :] < live_count[:, None]
    scores = jnp.where(live[None, :, None, :], scores, -1e30)
    highest = jnp.max(scores, axis=-1, keepdims=True)
    expo = jnp.exp(scores - highest)
    prob = expo / jnp.sum(expo, axis=-1, keepdims=True)
    prob_bf = prob.astype(jnp.bfloat16)
    attended = jnp.einsum(
        "hiqk,ikhd->iqhd", prob_bf, value_near, preferred_element_type=jnp.float32
    ).astype(jnp.bfloat16)
    return (prob, prob_bf, attended, key_near, value_near)


def backward(query_blk, links, grad_blk, prob, prob_bf, attended, key_near, value_near):
    scale = HD ** (-0.5)
    blocks = query_blk.shape[0]
    heads = query_blk.shape[2]
    value_part = jnp.einsum(
        "hiqk,iqhd->ikhd", prob_bf, grad_blk, preferred_element_type=jnp.float32
    )
    grad_prob = jnp.einsum(
        "iqhd,ikhd->hiqk", grad_blk, value_near, preferred_element_type=jnp.float32
    )
    delta = jnp.einsum("iqhd,iqhd->hiq", grad_blk, attended, preferred_element_type=jnp.float32)
    score_grad = (prob * (grad_prob - delta[..., None]) * scale).astype(jnp.bfloat16)
    query_grad = jnp.einsum(
        "hiqk,ikhd->iqhd", score_grad, key_near, preferred_element_type=jnp.float32
    ).astype(jnp.bfloat16)
    key_part = jnp.einsum(
        "hiqk,iqhd->ikhd", score_grad, query_blk, preferred_element_type=jnp.float32
    )
    member = (links.reshape(-1)[None, :] == jnp.arange(blocks)[:, None]).astype(jnp.float32)
    key_grad = jnp.einsum(
        "ja,aqhd->jqhd",
        member,
        key_part.reshape(blocks * NBR, BLK, heads, HD),
        precision=lax.Precision.HIGHEST,
    )
    value_grad = jnp.einsum(
        "ja,aqhd->jqhd",
        member,
        value_part.reshape(blocks * NBR, BLK, heads, HD),
        precision=lax.Precision.HIGHEST,
    )
    return (query_grad, key_grad.astype(jnp.bfloat16), value_grad.astype(jnp.bfloat16))


def local(queries, key_rows, values, adjacency, counts, out_weight, out_cotangent):
    query_heads, key_heads, value_heads = (
        lax.all_to_all(queries[0], "seq", split_axis=1, concat_axis=0, tiled=True),
        lax.all_to_all(key_rows[0], "seq", split_axis=1, concat_axis=0, tiled=True),
        lax.all_to_all(values[0], "seq", split_axis=1, concat_axis=0, tiled=True),
    )
    length = query_heads.shape[0]
    blocks = length // BLK
    heads = query_heads.shape[1] // HD
    shape = (blocks, BLK, heads, HD)
    links = adjacency[0]
    live_count = counts[0]
    query_blk = query_heads.reshape(shape)
    prob, prob_bf, attended, key_near, value_near = attend(
        query_blk, key_heads.reshape(shape), value_heads.reshape(shape), links, live_count
    )
    attn_tokens = lax.all_to_all(
        attended.reshape(length, heads * HD), "seq", split_axis=0, concat_axis=1, tiled=True
    )
    cotangent = out_cotangent[0]
    columns = attn_tokens
    layer_out = jnp.dot(
        columns,
        lax.all_gather(out_weight, "dp", axis=0, tiled=True),
        preferred_element_type=jnp.float32,
    )
    grad_tokens = lax.dot_general(
        cotangent,
        lax.all_gather(out_weight, "dp", axis=0, tiled=True),
        (((1,), (1,)), ((), ())),
        preferred_element_type=jnp.float32,
    )
    grad_heads = lax.all_to_all(
        grad_tokens.astype(jnp.bfloat16), "seq", split_axis=1, concat_axis=0, tiled=True
    )
    query_grad, key_grad, value_grad = backward(
        query_blk, links, grad_heads.reshape(shape), prob, prob_bf, attended, key_near, value_near
    )
    query_back, key_back, value_back = (
        lax.all_to_all(
            query_grad.reshape(length, heads * HD), "seq", split_axis=0, concat_axis=1, tiled=True
        ),
        lax.all_to_all(
            key_grad.reshape(length, heads * HD), "seq", split_axis=0, concat_axis=1, tiled=True
        ),
        lax.all_to_all(
            value_grad.reshape(length, heads * HD), "seq", split_axis=0, concat_axis=1, tiled=True
        ),
    )
    columns = attn_tokens
    weight_grad = lax.psum_scatter(
        lax.dot_general(
            columns, cotangent, (((0,), (0,)), ((), ())), preferred_element_type=jnp.float32
        ),
        ("dp", "seq"),
        scatter_dimension=0,
        tiled=True,
    )
    return (
        layer_out.astype(jnp.bfloat16)[None],
        query_back[None],
        key_back[None],
        value_back[None],
        weight_grad,
    )


def prep_kernel(n, per, q_ref, k_ref, v_ref, c_ref, w_ref, *rest):
    qkv, (same, other, wsend, sems) = by_slot(rest[:-4], n), rest[-4:]
    s = lax.axis_index("seq")
    core = s % 2
    half = c_ref.shape[2] // 2
    moves = []
    for j in range(n):
        for t, src in enumerate((q_ref, k_ref, v_ref)):
            for g in range(per):
                col = col_of(s ^ j, g, n // 2, per)
                moves.append((src.at[0, :, pl.ds(col, HD)], qkv[j].at[t, :, pl.ds(g * HD, HD)]))
    mine = pl.multiple_of(core * half, half)
    theirs = pl.multiple_of((1 - core) * half, half)
    moves.append((c_ref.at[0, :, pl.ds(mine, half)], same))
    moves.append((c_ref.at[0, :, pl.ds(theirs, half)], other))
    row = pl.multiple_of((s // 2) * HD, HD)
    moves.append((w_ref.at[pl.ds(row, HD), pl.ds(mine, half)], wsend))
    copies(moves, sems)


def order(n):
    return sorted(range(1, n), key=lambda j: (j == 1, j % 2, -j.bit_count(), j))


def by_slot(refs, n):
    slots = dict(zip([0] + order(n), refs))
    return [slots[j] for j in range(n)]


def stack_kernel(first_ref, second_ref, out_ref):
    rows = first_ref.shape[0]
    out_ref[:rows] = first_ref[...]
    out_ref[rows:] = second_ref[...]


def forward_kernel(n, per, adj_ref, cnt_ref, *rest):
    qkv, rest = by_slot(rest[:-11], n), rest[-11:]
    attn_ref, swap_ref, attn_t_ref, expo, share_ref, queries, keys_t, vals, keys, vals_t, score = rest
    s = lax.axis_index("seq")
    length = n * BLK
    tile = 2 * BLK
    scale = HD**-0.5 * LOG2E
    place = lax.broadcasted_iota(jnp.int32, (n, BLK), 0)
    biases = []
    for i in range(n):
        block = s ^ i
        count = cnt_ref[0, block]
        bias = jnp.full((n, BLK), DEAD, F32)
        for slot in range(NBR):
            j = jnp.where(slot < count, adj_ref[0, block, slot] ^ s, n)
            bias = jnp.where(place == j, 0.0, bias)
        biases.append(bias)
    for g in range(per):
        lanes = slice(g * HD, (g + 1) * HD)
        for j in range(n):
            rows = slice(j * BLK, (j + 1) * BLK)
            queries[g, rows, :] = qkv[j][0, :, lanes]
            key, val = qkv[j][1, :, lanes], qkv[j][2, :, lanes]
            keys[rows, :] = key
            keys_t[g, :, rows] = key.T
            vals[g, rows, :] = val
            vals_t[:, rows] = val.T
        for t in range(length // tile):
            cols = slice(t * tile, (t + 1) * tile)
            bias = jnp.concatenate(biases[2 * t : 2 * t + 2], axis=1)
            query = queries[g, cols, :]
            highest = jnp.full((1, tile), -jnp.inf, F32)
            for j in range(n):
                rows = slice(j * BLK, (j + 1) * BLK)
                part = mm(keys[rows, :], query, NT) * scale + bias[j : j + 1]
                score[rows, :] = part
                highest = jnp.maximum(highest, jnp.max(part, axis=0, keepdims=True))
            total = jnp.zeros((1, tile), F32)
            for j in range(n):
                rows = slice(j * BLK, (j + 1) * BLK)
                part = jnp.exp2(score[rows, :] - highest)
                total = total + jnp.sum(part, axis=0, keepdims=True)
                expo[g, rows, cols] = part.astype(BF16)
            share = 1.0 / total
            share_ref[g : g + 1, cols] = share
            att = (mm(vals_t[...], expo[g, :, cols]) * share).astype(BF16)
            attn_t_ref[g, :, cols] = att
            first, second = att[:, :BLK].T, att[:, BLK:].T
            base = t * tile
            attn_ref[base : base + BLK, lanes] = first
            attn_ref[base + BLK : base + tile, lanes] = second
            swap_ref[base : base + BLK, lanes] = second
            swap_ref[base + BLK : base + tile, lanes] = first


def grow_kernel(bit, mine_ref, recv_ref, out_ref):
    here = lax.axis_index("dp") // bit % 2
    for i in range(mine_ref.shape[0]):
        out_ref[2 * i + here] = mine_ref[i]
        out_ref[2 * i + 1 - here] = recv_ref[i]


def halve(total, bit, keep_ref, send_ref):
    here = lax.axis_index("dp") // bit % 2
    for i in range(keep_ref.shape[0]):
        keep_ref[i] = jnp.where(here == 0, total[2 * i], total[2 * i + 1])
        send_ref[i] = jnp.where(here == 0, total[2 * i + 1], total[2 * i]).astype(BF16)


def fold_kernel(bit, mine_ref, recv_ref, keep_ref, send_ref):
    halve(mine_ref[...] + recv_ref[...].astype(F32), bit, keep_ref, send_ref)


def grad_attn_kernel(n, per, *rest):
    cot, rest = rest[:-4], rest[-4:]
    w_ref, own_ref, send_ref, cot_out = rest
    core = lax.axis_index("seq") % 2
    mine = w_ref[pl.ds(pl.multiple_of(core * per * HD, HD), per * HD), :]
    theirs = w_ref[pl.ds(pl.multiple_of((1 - core) * per * HD, HD), per * HD), :]
    rows = n * BLK // len(cot)
    for j, ref in enumerate(cot):
        cot_out[j * rows : (j + 1) * rows, :] = ref[...]
    for t in range(n // 2):
        base = 2 * t * BLK
        rows = cot_out[base : base + 2 * BLK, :]
        own_ref[:, base : base + 2 * BLK] = mm(mine, rows, NT)
        part = mm(theirs, rows, NT).astype(BF16)
        send_ref[:, base : base + BLK] = part[:, BLK:]
        send_ref[:, base + BLK : base + 2 * BLK] = part[:, :BLK]


def backward_kernel(n, per, expo, share_ref, queries, keys_t, vals, attn_t_ref, own_ref, recv_ref, *rest):
    outs, (dscores,) = by_slot(rest[:-1], n), rest[-1:]
    scale = HD**-0.5
    tile = 2 * BLK
    length = n * BLK
    for g in range(per):
        lanes = slice(g * HD, (g + 1) * HD)
        full = (own_ref[lanes, :] + recv_ref[lanes, :].astype(F32)) * share_ref[g : g + 1, :]
        grad = full.astype(BF16)
        delta = jnp.sum(full * attn_t_ref[g].astype(F32), axis=0, keepdims=True)
        for t in range(length // tile):
            cols = slice(t * tile, (t + 1) * tile)
            dprob = mm(vals[g], grad[:, cols])
            dscores[:, cols] = (expo[g, :, cols].astype(F32) * (dprob - delta[:, cols])).astype(BF16)
        for t in range(length // tile):
            rows = slice(t * tile, (t + 1) * tile)
            dvalue = mm(expo[g, rows, :], grad, NT).astype(BF16)
            dkey = (mm(dscores[rows, :], queries[g]) * scale).astype(BF16)
            dquery = (mm(keys_t[g], dscores[:, rows]).T * scale).astype(BF16)
            for b in range(2):
                part = slice(b * BLK, (b + 1) * BLK)
                outs[2 * t + b][0, :, lanes] = dquery[part]
                outs[2 * t + b][1, :, lanes] = dkey[part]
                outs[2 * t + b][2, :, lanes] = dvalue[part]


def out_kernel(n, attn_ref, recv_ref, w_ref, *outs):
    core = lax.axis_index("seq") % 2
    tile = 2 * BLK
    heads = attn_ref.shape[1]
    mine = w_ref[pl.ds(pl.multiple_of(core * heads, heads), heads), :]
    theirs = w_ref[pl.ds(pl.multiple_of((1 - core) * heads, heads), heads), :]
    for t in range(n // 2):
        rows = slice(t * tile, (t + 1) * tile)
        part = mm(attn_ref[rows, :], mine) + mm(recv_ref[rows, :], theirs)
        if t < 3:
            outs[t][...] = part.astype(outs[t].dtype)
        else:
            outs[3][...] = part[:BLK].astype(BF16)
            outs[4][...] = part[BLK:].astype(BF16)


def relay_kernel(first_ref, first_recv, second_ref, second_recv, *outs):
    outs[0][:BLK] = first_ref[:BLK]
    outs[0][BLK:] = (first_ref[BLK:].astype(F32) + second_recv[...].astype(F32)).astype(BF16)
    outs[1][:BLK] = (second_ref[:BLK].astype(F32) + first_recv[...].astype(F32)).astype(BF16)
    outs[1][BLK:] = second_ref[BLK:]


def weight_kernel(per, attn_t_ref, recv_ref, cot_ref, keep_ref, send_ref, grads):
    core = lax.axis_index("seq") % 2
    for g in range(per):
        grads[core * per + g] = mm(attn_t_ref[g], cot_ref[...])
        recv = recv_ref[:, g * HD : (g + 1) * HD].T
        grads[(1 - core) * per + g] = mm(recv, cot_ref[...])
    halve(grads, 1, keep_ref, send_ref)


def out_sum_kernel(own_ref, *rest):
    parts, (keep_ref, send_ref) = rest[:-2], rest[-2:]
    total = own_ref[...]
    for part in parts:
        total = total + part[...].astype(F32)
    total = total.astype(BF16)
    keep_ref[...] = total[:BLK]
    send_ref[...] = total[BLK:]


def weight_sum_kernel(own_ref, recv_ref, keep_ref, send_ref):
    total = own_ref[0] + recv_ref[0].astype(F32)
    half = total.shape[0] // 2
    core = lax.axis_index("seq") % 2
    keep_ref[...] = jnp.where(core == 0, total[:half], total[half:])
    send_ref[...] = jnp.where(core == 0, total[half:], total[:half])


def place_kernel(n, per, keep_ref, recv_ref, w_keep_ref, w_recv_ref, *rest):
    parts, (out_ref, *outs, w_ref, sems) = by_slot(rest[:-6], n), rest[-6:]
    s = lax.axis_index("seq")
    core = s % 2
    half = keep_ref.shape[1]
    mine = pl.ds(pl.multiple_of(core * half, half), half)
    theirs = pl.ds(pl.multiple_of((1 - core) * half, half), half)
    moves = [
        (keep_ref, out_ref.at[0, :, mine]),
        (recv_ref, out_ref.at[0, :, theirs]),
        (w_keep_ref, w_ref.at[:, mine]),
        (w_recv_ref, w_ref.at[:, theirs]),
    ]
    for g in range(per):
        for j in range(n):
            col = col_of(s ^ j, g, n // 2, per)
            for t in range(3):
                src = parts[j].at[t, :, pl.ds(g * HD, HD)]
                moves.append((src, outs[t].at[0, :, pl.ds(col, HD)]))
    copies(moves, sems)


def paired(n, nz, queries, key_rows, values, adjacency, counts, out_weight, out_cotangent):
    per = nz // 2
    pairs = n // 2
    length = n * BLK
    wide = queries.shape[2]
    half = wide // 2
    heads = per * HD
    chunk = sds((3, BLK, heads), BF16)
    piece = sds((BLK, half), BF16)
    couple = sds((2 * BLK, half), BF16)

    def to(x, j):
        return lax.ppermute(x, "seq", [(i, i ^ j) for i in range(n)])

    def to_z(x, j):
        return lax.ppermute(x, "dp", [(i, i ^ j) for i in range(nz)])

    def exchange(parts):
        return [parts[0]] + [to(part, j) for part, j in zip(parts[1:], order(n))]

    prep = call(
        functools.partial(prep_kernel, n, per),
        [(HBM, in_hbm(x)) for x in (queries, key_rows, values, out_cotangent, out_weight)],
        [(VMEM, pltpu.VMEM(x.shape, x.dtype)) for x in [chunk] * n + [piece] * 3],
        [pltpu.SemaphoreType.DMA((3 * n * per + 3,))],
        moved=8 * MIB,
    )
    same, other, w_own = prep[n:]
    qkv = exchange(prep[:n])
    (cot_own,) = call(
        stack_kernel, [(VMEM, same), (VMEM, to(other, 1))], [(VMEM, couple)], moved=MIB
    )
    sent = dict(zip(order(n), qkv[1:]))
    cot_sent = after(cot_own, *[sent[j] for j in order(n)[: pairs - 1]])
    cot = [cot_own] + [to(cot_sent, 2 * jc) for jc in range(1, pairs)]
    w_rows = w_own[None]
    bit = nz
    while bit > 1:
        bit //= 2
        (w_rows,) = call(
            functools.partial(grow_kernel, bit),
            [(VMEM, w_rows), (VMEM, to_z(w_rows, bit))],
            [(VMEM, sds((2 * w_rows.shape[0], HD, half), BF16))],
            moved=2 * MIB,
        )
    w_rows = w_rows.reshape(nz * HD, half)

    attn, swap, attn_t, *kept = call(
        functools.partial(forward_kernel, n, per),
        [(SMEM, adjacency), (SMEM, counts)] + [(VMEM, x) for x in qkv],
        [
            (VMEM, sds((length, heads), BF16)),
            (VMEM, sds((length, heads), BF16)),
            (VMEM, sds((per, HD, length), BF16)),
            (VMEM, sds((per, length, length), BF16)),
            (VMEM, sds((per, length), F32)),
            (VMEM, sds((per, length, HD), BF16)),
            (VMEM, sds((per, HD, length), BF16)),
            (VMEM, sds((per, length, HD), BF16)),
        ],
        [
            pltpu.VMEM((length, HD), BF16),
            pltpu.VMEM((HD, length), BF16),
            pltpu.VMEM((length, 2 * BLK), F32),
        ],
        flops=4 * per * length * length * HD,
        moved=8 * MIB,
    )
    attn_recv = to(swap, 1)

    grad_own, grad_send, cot_rows = call(
        functools.partial(grad_attn_kernel, n, per),
        [(VMEM, x) for x in cot + [w_rows]],
        [
            (VMEM, sds((heads, length), F32)),
            (VMEM, sds((heads, length), BF16)),
            (VMEM, sds((length, half), BF16)),
        ],
        flops=4 * length * heads * half,
        moved=8 * MIB,
    )
    grad_recv = to(grad_send, 1)
    out_own, out_x, out_y, out_far_x, out_far_y = call(
        functools.partial(out_kernel, n),
        [(VMEM, attn), (VMEM, attn_recv), (VMEM, after(w_rows, grad_own))],
        [(VMEM, x) for x in (sds((2 * BLK, half), F32), couple, couple, piece, piece)],
        flops=4 * length * heads * half,
        moved=6 * MIB,
    )
    far_x, far_y = to(out_far_x, 2), to(out_far_y, 4)
    w_keep, w_send = call(
        functools.partial(weight_kernel, per),
        [(VMEM, attn_t), (VMEM, attn_recv), (VMEM, cot_rows)],
        [(VMEM, sds((per, HD, half), d)) for d in (F32, BF16)],
        [pltpu.VMEM((nz, HD, half), F32)],
        flops=4 * length * heads * half,
        moved=6 * MIB,
    )
    grads = call(
        functools.partial(backward_kernel, n, per),
        [(VMEM, x) for x in kept + [attn_t, after(grad_own, w_keep, out_own), grad_recv]],
        [(VMEM, chunk)] * n,
        [pltpu.VMEM((length, length), BF16)],
        flops=8 * per * length * length * HD,
        moved=8 * MIB,
    )
    relayed = call(
        relay_kernel,
        [(VMEM, x) for x in (after(out_x, grads[0]), far_x, out_y, far_y)],
        [(VMEM, couple)] * 2,
        moved=3 * MIB,
    )
    out_recv = [to(relayed[0], 2), to(relayed[1], 4)]
    back = exchange(grads)

    bit = 1
    while 2 * bit < nz:
        w_keep, w_send = call(
            functools.partial(fold_kernel, 2 * bit),
            [(VMEM, w_keep), (VMEM, to_z(w_send, bit))],
            [(VMEM, sds((w_keep.shape[0] // 2, HD, half), d)) for d in (F32, BF16)],
            moved=2 * MIB,
        )
        bit *= 2
    w_recv = to_z(w_send, bit)

    out_keep, out_send = call(
        out_sum_kernel,
        [(VMEM, x) for x in [after(out_own, grads[0])] + out_recv],
        [(VMEM, piece)] * 2,
        moved=3 * MIB,
    )
    half_keep, half_send = call(
        weight_sum_kernel,
        [(VMEM, after(w_keep, out_keep, back[1])), (VMEM, w_recv)],
        [(VMEM, sds((HD // 2, half), F32))] * 2,
        moved=2 * MIB,
    )
    token = sds((1, BLK, wide), BF16)
    return call(
        functools.partial(place_kernel, n, per),
        [(ANY, x) for x in [out_keep, to(out_send, 1), half_keep, to(half_send, 1)] + back],
        [(ANY, token)] * 4 + [(ANY, sds((HD // 2, wide), F32))],
        [pltpu.SemaphoreType.DMA((3 * n * per + 4,))],
        moved=4 * MIB,
    )


def solution(mesh):
    in_specs = (
        P("dp", "seq", None),
        P("dp", "seq", None),
        P("dp", "seq", None),
        P("dp", None, None),
        P("dp", None),
        P("dp", None),
        P("dp", "seq", None),
    )
    out_specs = (
        P("dp", "seq", None),
        P("dp", "seq", None),
        P("dp", "seq", None),
        P("dp", "seq", None),
        P(("dp", "seq"), None),
    )
    n, nz = mesh.shape["seq"], mesh.shape["dp"]

    def body(queries, *rest):
        fits = queries.shape[1] == BLK and queries.shape[2] == nz * (n // 2) * HD
        if fits and n == 8 and nz > 1 and nz & (nz - 1) == 0:
            return paired(n, nz, queries, *rest)
        return local(queries, *rest)

    return jax.shard_map(body, mesh=mesh, in_specs=in_specs, out_specs=out_specs, check_vma=False)
```

```python
import functools

import jax
import jax.numpy as jnp
from jax import lax
from jax.experimental import pallas as pl
from jax.experimental.pallas import tpu as pltpu
from jax.sharding import PartitionSpec as P

HD = 128
BLK = 128
NBR = 8
F32 = jnp.float32
BF16 = jnp.bfloat16
NN = (((1,), (0,)), ((), ()))
NT = (((1,), (1,)), ((), ()))
LOG2E = 1.4426950408889634
DEAD = -1e30
VMEM = pl.BlockSpec(memory_space=pltpu.VMEM)
SMEM = pl.BlockSpec(memory_space=pltpu.SMEM)
HBM = pl.BlockSpec(memory_space=pltpu.HBM)
ANY = pl.BlockSpec(memory_space=pl.ANY)
MIB = 1 << 20


def mm(a, b, dims=NN):
    return lax.dot_general(a, b, dims, preferred_element_type=F32)


def in_hbm(x):
    return pltpu.with_memory_space_constraint(x, pltpu.HBM)


def sds(shape, dtype):
    return jax.ShapeDtypeStruct(shape, dtype)


def after(x, *deps):
    return lax.optimization_barrier((x,) + deps)[0]


def call(kernel, ins, outs, scratch=(), flops=0, moved=0, vmem=24):
    return pl.pallas_call(
        kernel,
        out_shape=tuple(shape for _, shape in outs),
        in_specs=[spec for spec, _ in ins],
        out_specs=tuple(spec for spec, _ in outs),
        scratch_shapes=list(scratch),
        compiler_params=pltpu.CompilerParams(vmem_limit_bytes=vmem * MIB),
        cost_estimate=pl.CostEstimate(flops=flops, bytes_accessed=moved, transcendentals=0),
    )(*[arg for _, arg in ins])


def col_of(dev, g, pairs, per):
    return pl.multiple_of(((dev % 2 * per + g) * pairs + dev // 2) * HD, HD)


def attend(query_blk, key_blk, value_blk, links, live_count):
    scale = HD ** (-0.5)
    blocks = query_blk.shape[0]
    heads = query_blk.shape[2]
    key_near = key_blk[links].reshape(blocks, NBR * BLK, heads, HD)
    value_near = value_blk[links].reshape(blocks, NBR * BLK, heads, HD)
    scores = (
        jnp.einsum("iqhd,ikhd->hiqk", query_blk, key_near, preferred_element_type=jnp.float32)
        * scale
    )
    live = (jnp.arange(NBR * BLK) // BLK)[None, :] < live_count[:, None]
    scores = jnp.where(live[None, :, None, :], scores, -1e30)
    highest = jnp.max(scores, axis=-1, keepdims=True)
    expo = jnp.exp(scores - highest)
    prob = expo / jnp.sum(expo, axis=-1, keepdims=True)
    prob_bf = prob.astype(jnp.bfloat16)
    attended = jnp.einsum(
        "hiqk,ikhd->iqhd", prob_bf, value_near, preferred_element_type=jnp.float32
    ).astype(jnp.bfloat16)
    return (prob, prob_bf, attended, key_near, value_near)


def backward(query_blk, links, grad_blk, prob, prob_bf, attended, key_near, value_near):
    scale = HD ** (-0.5)
    blocks = query_blk.shape[0]
    heads = query_blk.shape[2]
    value_part = jnp.einsum(
        "hiqk,iqhd->ikhd", prob_bf, grad_blk, preferred_element_type=jnp.float32
    )
    grad_prob = jnp.einsum(
        "iqhd,ikhd->hiqk", grad_blk, value_near, preferred_element_type=jnp.float32
    )
    delta = jnp.einsum("iqhd,iqhd->hiq", grad_blk, attended, preferred_element_type=jnp.float32)
    score_grad = (prob * (grad_prob - delta[..., None]) * scale).astype(jnp.bfloat16)
    query_grad = jnp.einsum(
        "hiqk,ikhd->iqhd", score_grad, key_near, preferred_element_type=jnp.float32
    ).astype(jnp.bfloat16)
    key_part = jnp.einsum(
        "hiqk,iqhd->ikhd", score_grad, query_blk, preferred_element_type=jnp.float32
    )
    member = (links.reshape(-1)[None, :] == jnp.arange(blocks)[:, None]).astype(jnp.float32)
    key_grad = jnp.einsum(
        "ja,aqhd->jqhd",
        member,
        key_part.reshape(blocks * NBR, BLK, heads, HD),
        precision=lax.Precision.HIGHEST,
    )
    value_grad = jnp.einsum(
        "ja,aqhd->jqhd",
        member,
        value_part.reshape(blocks * NBR, BLK, heads, HD),
        precision=lax.Precision.HIGHEST,
    )
    return (query_grad, key_grad.astype(jnp.bfloat16), value_grad.astype(jnp.bfloat16))


def local(queries, key_rows, values, adjacency, counts, out_weight, out_cotangent):
    query_heads, key_heads, value_heads = (
        lax.all_to_all(queries[0], "seq", split_axis=1, concat_axis=0, tiled=True),
        lax.all_to_all(key_rows[0], "seq", split_axis=1, concat_axis=0, tiled=True),
        lax.all_to_all(values[0], "seq", split_axis=1, concat_axis=0, tiled=True),
    )
    length = query_heads.shape[0]
    blocks = length // BLK
    heads = query_heads.shape[1] // HD
    shape = (blocks, BLK, heads, HD)
    links = adjacency[0]
    live_count = counts[0]
    query_blk = query_heads.reshape(shape)
    prob, prob_bf, attended, key_near, value_near = attend(
        query_blk, key_heads.reshape(shape), value_heads.reshape(shape), links, live_count
    )
    attn_tokens = lax.all_to_all(
        attended.reshape(length, heads * HD), "seq", split_axis=0, concat_axis=1, tiled=True
    )
    cotangent = out_cotangent[0]
    columns = attn_tokens
    layer_out = jnp.dot(
        columns,
        lax.all_gather(out_weight, "dp", axis=0, tiled=True),
        preferred_element_type=jnp.float32,
    )
    grad_tokens = lax.dot_general(
        cotangent,
        lax.all_gather(out_weight, "dp", axis=0, tiled=True),
        (((1,), (1,)), ((), ())),
        preferred_element_type=jnp.float32,
    )
    grad_heads = lax.all_to_all(
        grad_tokens.astype(jnp.bfloat16), "seq", split_axis=1, concat_axis=0, tiled=True
    )
    query_grad, key_grad, value_grad = backward(
        query_blk, links, grad_heads.reshape(shape), prob, prob_bf, attended, key_near, value_near
    )
    query_back, key_back, value_back = (
        lax.all_to_all(
            query_grad.reshape(length, heads * HD), "seq", split_axis=0, concat_axis=1, tiled=True
        ),
        lax.all_to_all(
            key_grad.reshape(length, heads * HD), "seq", split_axis=0, concat_axis=1, tiled=True
        ),
        lax.all_to_all(
            value_grad.reshape(length, heads * HD), "seq", split_axis=0, concat_axis=1, tiled=True
        ),
    )
    columns = attn_tokens
    weight_grad = lax.psum_scatter(
        lax.dot_general(
            columns, cotangent, (((0,), (0,)), ((), ())), preferred_element_type=jnp.float32
        ),
        ("dp", "seq"),
        scatter_dimension=0,
        tiled=True,
    )
    return (
        layer_out.astype(jnp.bfloat16)[None],
        query_back[None],
        key_back[None],
        value_back[None],
        weight_grad,
    )


def prep_kernel(n, per, q_ref, k_ref, v_ref, c_ref, w_ref, *rest):
    qkv, (same, other, w_own, whole, sems) = by_slot(rest[:-5], n), rest[-5:]
    s = lax.axis_index("seq")
    core = s % 2
    half = c_ref.shape[2] // 2
    mine = pl.multiple_of(core * half, half)
    theirs = pl.multiple_of((1 - core) * half, half)
    row = pl.multiple_of((s // 2) * HD, HD)
    moves = [(src.at[0], whole.at[t]) for t, src in enumerate((q_ref, k_ref, v_ref))]
    moves.append((c_ref.at[0, :, pl.ds(mine, half)], same))
    moves.append((c_ref.at[0, :, pl.ds(theirs, half)], other))
    moves.append((w_ref.at[pl.ds(row, HD), pl.ds(mine, half)], w_own))
    handles = [pltpu.make_async_copy(src, dst, sems.at[m]) for m, (src, dst) in enumerate(moves)]
    for handle in handles:
        handle.start()
    for t in range(3):
        handles[t].wait()
        for j in range(n):
            for g in range(per):
                col = col_of(s ^ j, g, n // 2, per)
                qkv[j][t, :, g * HD : (g + 1) * HD] = whole[t, :, pl.ds(col, HD)]
    for handle in handles[3:]:
        handle.wait()


def order(n):
    return sorted(range(1, n), key=lambda j: (j == 1, j % 2, -j.bit_count(), j))


def by_slot(refs, n):
    slots = dict(zip([0] + order(n), refs))
    return [slots[j] for j in range(n)]


def stack_kernel(first_ref, second_ref, out_ref):
    rows = first_ref.shape[0]
    out_ref[:rows] = first_ref[...]
    out_ref[rows:] = second_ref[...]


def forward_kernel(n, per, adj_ref, cnt_ref, *rest):
    qkv, rest = by_slot(rest[:-11], n), rest[-11:]
    attn_ref, swap_ref, attn_t_ref, expo, share_ref, queries, keys_t, vals, keys, vals_t, score = rest
    s = lax.axis_index("seq")
    length = n * BLK
    tile = 2 * BLK
    scale = HD**-0.5 * LOG2E
    place = lax.broadcasted_iota(jnp.int32, (n, BLK), 0)
    biases = []
    for i in range(n):
        block = s ^ i
        count = cnt_ref[0, block]
        bias = jnp.full((n, BLK), DEAD, F32)
        for slot in range(NBR):
            j = jnp.where(slot < count, adj_ref[0, block, slot] ^ s, n)
            bias = jnp.where(place == j, 0.0, bias)
        biases.append(bias)
    for g in range(per):
        lanes = slice(g * HD, (g + 1) * HD)
        for j in range(n):
            rows = slice(j * BLK, (j + 1) * BLK)
            queries[g, rows, :] = qkv[j][0, :, lanes]
            key, val = qkv[j][1, :, lanes], qkv[j][2, :, lanes]
            keys[rows, :] = key
            keys_t[g, :, rows] = key.T
            vals[g, rows, :] = val
            vals_t[:, rows] = val.T
        for t in range(length // tile):
            cols = slice(t * tile, (t + 1) * tile)
            bias = jnp.concatenate(biases[2 * t : 2 * t + 2], axis=1)
            query = queries[g, cols, :]
            highest = jnp.full((1, tile), -jnp.inf, F32)
            for j in range(n):
                rows = slice(j * BLK, (j + 1) * BLK)
                part = mm(keys[rows, :], query, NT) * scale + bias[j : j + 1]
                score[rows, :] = part
                highest = jnp.maximum(highest, jnp.max(part, axis=0, keepdims=True))
            total = jnp.zeros((1, tile), F32)
            for j in range(n):
                rows = slice(j * BLK, (j + 1) * BLK)
                part = jnp.exp2(score[rows, :] - highest)
                total = total + jnp.sum(part, axis=0, keepdims=True)
                expo[g, rows, cols] = part.astype(BF16)
            share = 1.0 / total
            share_ref[g : g + 1, cols] = share
            att = (mm(vals_t[...], expo[g, :, cols]) * share).astype(BF16)
            attn_t_ref[g, :, cols] = att
            first, second = att[:, :BLK].T, att[:, BLK:].T
            base = t * tile
            attn_ref[base : base + BLK, lanes] = first
            attn_ref[base + BLK : base + tile, lanes] = second
            swap_ref[base : base + BLK, lanes] = second
            swap_ref[base + BLK : base + tile, lanes] = first


def grow_kernel(bit, mine_ref, recv_ref, out_ref):
    here = lax.axis_index("dp") // bit % 2
    for i in range(mine_ref.shape[0]):
        out_ref[2 * i + here] = mine_ref[i]
        out_ref[2 * i + 1 - here] = recv_ref[i]


def halve(total, bit, keep_ref, send_ref):
    here = lax.axis_index("dp") // bit % 2
    for i in range(keep_ref.shape[0]):
        keep_ref[i] = jnp.where(here == 0, total[2 * i], total[2 * i + 1])
        send_ref[i] = jnp.where(here == 0, total[2 * i + 1], total[2 * i]).astype(BF16)


def fold_kernel(bit, mine_ref, recv_ref, keep_ref, send_ref):
    halve(mine_ref[...] + recv_ref[...].astype(F32), bit, keep_ref, send_ref)


def grad_attn_kernel(n, per, *rest):
    cot, rest = rest[:-4], rest[-4:]
    w_ref, own_ref, send_ref, cot_out = rest
    core = lax.axis_index("seq") % 2
    mine = w_ref[pl.ds(pl.multiple_of(core * per * HD, HD), per * HD), :]
    theirs = w_ref[pl.ds(pl.multiple_of((1 - core) * per * HD, HD), per * HD), :]
    rows = n * BLK // len(cot)
    for j, ref in enumerate(cot):
        cot_out[j * rows : (j + 1) * rows, :] = ref[...]
    for t in range(n // 2):
        base = 2 * t * BLK
        rows = cot_out[base : base + 2 * BLK, :]
        own_ref[:, base : base + 2 * BLK] = mm(mine, rows, NT)
        part = mm(theirs, rows, NT).astype(BF16)
        send_ref[:, base : base + BLK] = part[:, BLK:]
        send_ref[:, base + BLK : base + 2 * BLK] = part[:, :BLK]


def backward_kernel(n, per, expo, share_ref, queries, keys_t, vals, attn_t_ref, own_ref, recv_ref, *rest):
    outs, (dscores,) = by_slot(rest[:-1], n), rest[-1:]
    scale = HD**-0.5
    tile = 2 * BLK
    length = n * BLK
    for g in range(per):
        lanes = slice(g * HD, (g + 1) * HD)
        full = (own_ref[lanes, :] + recv_ref[lanes, :].astype(F32)) * share_ref[g : g + 1, :]
        grad = full.astype(BF16)
        delta = jnp.sum(full * attn_t_ref[g].astype(F32), axis=0, keepdims=True)
        for t in range(length // tile):
            cols = slice(t * tile, (t + 1) * tile)
            dprob = mm(vals[g], grad[:, cols])
            dscores[:, cols] = (expo[g, :, cols].astype(F32) * (dprob - delta[:, cols])).astype(BF16)
        for t in range(length // tile):
            rows = slice(t * tile, (t + 1) * tile)
            dvalue = mm(expo[g, rows, :], grad, NT).astype(BF16)
            dkey = (mm(dscores[rows, :], queries[g]) * scale).astype(BF16)
            dquery = (mm(keys_t[g], dscores[:, rows]).T * scale).astype(BF16)
            for b in range(2):
                part = slice(b * BLK, (b + 1) * BLK)
                outs[2 * t + b][0, :, lanes] = dquery[part]
                outs[2 * t + b][1, :, lanes] = dkey[part]
                outs[2 * t + b][2, :, lanes] = dvalue[part]


def out_kernel(n, attn_ref, recv_ref, w_ref, *outs):
    core = lax.axis_index("seq") % 2
    tile = 2 * BLK
    heads = attn_ref.shape[1]
    mine = w_ref[pl.ds(pl.multiple_of(core * heads, heads), heads), :]
    theirs = w_ref[pl.ds(pl.multiple_of((1 - core) * heads, heads), heads), :]
    for t in range(n // 2):
        rows = slice(t * tile, (t + 1) * tile)
        part = mm(attn_ref[rows, :], mine) + mm(recv_ref[rows, :], theirs)
        if t < 3:
            outs[t][...] = part.astype(outs[t].dtype)
        else:
            outs[3][...] = part[:BLK].astype(BF16)
            outs[4][...] = part[BLK:].astype(BF16)


def relay_kernel(first_ref, first_recv, second_ref, second_recv, *outs):
    outs[0][:BLK] = first_ref[:BLK]
    outs[0][BLK:] = (first_ref[BLK:].astype(F32) + second_recv[...].astype(F32)).astype(BF16)
    outs[1][:BLK] = (second_ref[:BLK].astype(F32) + first_recv[...].astype(F32)).astype(BF16)
    outs[1][BLK:] = second_ref[BLK:]


def weight_kernel(per, attn_t_ref, recv_ref, cot_ref, keep_ref, send_ref, grads):
    core = lax.axis_index("seq") % 2
    for g in range(per):
        grads[core * per + g] = mm(attn_t_ref[g], cot_ref[...])
        recv = recv_ref[:, g * HD : (g + 1) * HD].T
        grads[(1 - core) * per + g] = mm(recv, cot_ref[...])
    halve(grads, 1, keep_ref, send_ref)


def out_sum_kernel(own_ref, *rest):
    parts, (keep_ref, send_ref) = rest[:-2], rest[-2:]
    total = own_ref[...]
    for part in parts:
        total = total + part[...].astype(F32)
    total = total.astype(BF16)
    keep_ref[...] = total[:BLK]
    send_ref[...] = total[BLK:]


def weight_sum_kernel(own_ref, recv_ref, keep_ref, send_ref):
    total = own_ref[0] + recv_ref[0].astype(F32)
    half = total.shape[0] // 2
    core = lax.axis_index("seq") % 2
    keep_ref[...] = jnp.where(core == 0, total[:half], total[half:])
    send_ref[...] = jnp.where(core == 0, total[half:], total[:half])


def place_kernel(n, per, keep_ref, recv_ref, w_keep_ref, w_recv_ref, *rest):
    parts, (out_ref, *outs, w_ref, whole, sems) = by_slot(rest[:-7], n), rest[-7:]
    s = lax.axis_index("seq")
    core = s % 2
    half = keep_ref.shape[1]
    mine = pl.ds(pl.multiple_of(core * half, half), half)
    theirs = pl.ds(pl.multiple_of((1 - core) * half, half), half)
    moves = [
        (keep_ref, out_ref.at[0, :, mine]),
        (recv_ref, out_ref.at[0, :, theirs]),
        (w_keep_ref, w_ref.at[:, mine]),
        (w_recv_ref, w_ref.at[:, theirs]),
    ]
    moves += [(whole.at[t], outs[t].at[0]) for t in range(3)]
    handles = [pltpu.make_async_copy(src, dst, sems.at[m]) for m, (src, dst) in enumerate(moves)]
    for handle in handles[:4]:
        handle.start()
    for t in range(3):
        for j in range(n):
            for g in range(per):
                col = col_of(s ^ j, g, n // 2, per)
                whole[t, :, pl.ds(col, HD)] = parts[j][t, :, g * HD : (g + 1) * HD]
        handles[4 + t].start()
    for handle in handles:
        handle.wait()


def paired(n, nz, queries, key_rows, values, adjacency, counts, out_weight, out_cotangent):
    per = nz // 2
    pairs = n // 2
    length = n * BLK
    wide = queries.shape[2]
    half = wide // 2
    heads = per * HD
    chunk = sds((3, BLK, heads), BF16)
    piece = sds((BLK, half), BF16)
    couple = sds((2 * BLK, half), BF16)

    def to(x, j):
        return lax.ppermute(x, "seq", [(i, i ^ j) for i in range(n)])

    def to_z(x, j):
        return lax.ppermute(x, "dp", [(i, i ^ j) for i in range(nz)])

    def exchange(parts):
        return [parts[0]] + [to(part, j) for part, j in zip(parts[1:], order(n))]

    prep = call(
        functools.partial(prep_kernel, n, per),
        [(HBM, in_hbm(x)) for x in (queries, key_rows, values, out_cotangent, out_weight)],
        [(VMEM, pltpu.VMEM(x.shape, x.dtype)) for x in [chunk] * n + [piece] * 3],
        [pltpu.VMEM((3, BLK, wide), BF16), pltpu.SemaphoreType.DMA((6,))],
        moved=8 * MIB,
    )
    same, other, w_own = prep[n:]
    qkv = exchange(prep[:n])
    (cot_own,) = call(
        stack_kernel, [(VMEM, same), (VMEM, to(other, 1))], [(VMEM, couple)], moved=MIB
    )
    sent = dict(zip(order(n), qkv[1:]))
    cot_sent = after(cot_own, *[sent[j] for j in order(n)[: pairs - 1]])
    cot = [cot_own] + [to(cot_sent, 2 * jc) for jc in range(1, pairs)]
    w_rows = w_own[None]
    bit = nz
    while bit > 1:
        bit //= 2
        (w_rows,) = call(
            functools.partial(grow_kernel, bit),
            [(VMEM, w_rows), (VMEM, to_z(w_rows, bit))],
            [(VMEM, sds((2 * w_rows.shape[0], HD, half), BF16))],
            moved=2 * MIB,
        )
    w_rows = w_rows.reshape(nz * HD, half)

    attn, swap, attn_t, *kept = call(
        functools.partial(forward_kernel, n, per),
        [(SMEM, adjacency), (SMEM, counts)] + [(VMEM, x) for x in qkv],
        [
            (VMEM, sds((length, heads), BF16)),
            (VMEM, sds((length, heads), BF16)),
            (VMEM, sds((per, HD, length), BF16)),
            (VMEM, sds((per, length, length), BF16)),
            (VMEM, sds((per, length), F32)),
            (VMEM, sds((per, length, HD), BF16)),
            (VMEM, sds((per, HD, length), BF16)),
            (VMEM, sds((per, length, HD), BF16)),
        ],
        [
            pltpu.VMEM((length, HD), BF16),
            pltpu.VMEM((HD, length), BF16),
            pltpu.VMEM((length, 2 * BLK), F32),
        ],
        flops=4 * per * length * length * HD,
        moved=8 * MIB,
    )
    attn_recv = to(swap, 1)

    grad_own, grad_send, cot_rows = call(
        functools.partial(grad_attn_kernel, n, per),
        [(VMEM, x) for x in cot + [w_rows]],
        [
            (VMEM, sds((heads, length), F32)),
            (VMEM, sds((heads, length), BF16)),
            (VMEM, sds((length, half), BF16)),
        ],
        flops=4 * length * heads * half,
        moved=8 * MIB,
    )
    grad_recv = to(grad_send, 1)
    out_own, out_x, out_y, out_far_x, out_far_y = call(
        functools.partial(out_kernel, n),
        [(VMEM, attn), (VMEM, attn_recv), (VMEM, after(w_rows, grad_own))],
        [(VMEM, x) for x in (sds((2 * BLK, half), F32), couple, couple, piece, piece)],
        flops=4 * length * heads * half,
        moved=6 * MIB,
    )
    far_x, far_y = to(out_far_x, 2), to(out_far_y, 4)
    w_keep, w_send = call(
        functools.partial(weight_kernel, per),
        [(VMEM, attn_t), (VMEM, attn_recv), (VMEM, cot_rows)],
        [(VMEM, sds((per, HD, half), d)) for d in (F32, BF16)],
        [pltpu.VMEM((nz, HD, half), F32)],
        flops=4 * length * heads * half,
        moved=6 * MIB,
    )
    grads = call(
        functools.partial(backward_kernel, n, per),
        [(VMEM, x) for x in kept + [attn_t, after(grad_own, w_keep, out_own), grad_recv]],
        [(VMEM, chunk)] * n,
        [pltpu.VMEM((length, length), BF16)],
        flops=8 * per * length * length * HD,
        moved=8 * MIB,
    )
    relayed = call(
        relay_kernel,
        [(VMEM, x) for x in (after(out_x, grads[0]), far_x, out_y, far_y)],
        [(VMEM, couple)] * 2,
        moved=3 * MIB,
    )
    out_recv = [to(relayed[0], 2), to(relayed[1], 4)]
    back = exchange(grads)

    bit = 1
    while 2 * bit < nz:
        w_keep, w_send = call(
            functools.partial(fold_kernel, 2 * bit),
            [(VMEM, w_keep), (VMEM, to_z(w_send, bit))],
            [(VMEM, sds((w_keep.shape[0] // 2, HD, half), d)) for d in (F32, BF16)],
            moved=2 * MIB,
        )
        bit *= 2
    w_recv = to_z(w_send, bit)

    out_keep, out_send = call(
        out_sum_kernel,
        [(VMEM, x) for x in [after(out_own, grads[0])] + out_recv],
        [(VMEM, piece)] * 2,
        moved=3 * MIB,
    )
    half_keep, half_send = call(
        weight_sum_kernel,
        [(VMEM, after(w_keep, out_keep, back[1])), (VMEM, w_recv)],
        [(VMEM, sds((HD // 2, half), F32))] * 2,
        moved=2 * MIB,
    )
    token = sds((1, BLK, wide), BF16)
    return call(
        functools.partial(place_kernel, n, per),
        [(VMEM, x) for x in [out_keep, to(out_send, 1), half_keep, to(half_send, 1)] + back],
        [(ANY, token)] * 4 + [(ANY, sds((HD // 2, wide), F32))],
        [pltpu.VMEM((3, BLK, wide), BF16), pltpu.SemaphoreType.DMA((7,))],
        moved=4 * MIB,
    )


def solution(mesh):
    in_specs = (
        P("dp", "seq", None),
        P("dp", "seq", None),
        P("dp", "seq", None),
        P("dp", None, None),
        P("dp", None),
        P("dp", None),
        P("dp", "seq", None),
    )
    out_specs = (
        P("dp", "seq", None),
        P("dp", "seq", None),
        P("dp", "seq", None),
        P("dp", "seq", None),
        P(("dp", "seq"), None),
    )
    n, nz = mesh.shape["seq"], mesh.shape["dp"]

    def body(queries, *rest):
        fits = queries.shape[1] == BLK and queries.shape[2] == nz * (n // 2) * HD
        if fits and n == 8 and nz > 1 and nz & (nz - 1) == 0:
            return paired(n, nz, queries, *rest)
        return local(queries, *rest)

    return jax.shard_map(body, mesh=mesh, in_specs=in_specs, out_specs=out_specs, check_vma=False)
```

```python
import functools

import jax
import jax.numpy as jnp
from jax import lax
from jax.experimental import pallas as pl
from jax.experimental.pallas import tpu as pltpu
from jax.sharding import PartitionSpec as P

HD = 128
BLK = 128
NBR = 8
F32 = jnp.float32
BF16 = jnp.bfloat16
NN = (((1,), (0,)), ((), ()))
NT = (((1,), (1,)), ((), ()))
LOG2E = 1.4426950408889634
DEAD = -1e30
VMEM = pl.BlockSpec(memory_space=pltpu.VMEM)
SMEM = pl.BlockSpec(memory_space=pltpu.SMEM)
HBM = pl.BlockSpec(memory_space=pltpu.HBM)
ANY = pl.BlockSpec(memory_space=pl.ANY)
MIB = 1 << 20


def mm(a, b, dims=NN):
    return lax.dot_general(a, b, dims, preferred_element_type=F32)


def in_hbm(x):
    return pltpu.with_memory_space_constraint(x, pltpu.HBM)


def sds(shape, dtype):
    return jax.ShapeDtypeStruct(shape, dtype)


def after(x, *deps):
    return lax.optimization_barrier((x,) + deps)[0]


def call(kernel, ins, outs, scratch=(), flops=0, moved=0, vmem=24):
    return pl.pallas_call(
        kernel,
        out_shape=tuple(shape for _, shape in outs),
        in_specs=[spec for spec, _ in ins],
        out_specs=tuple(spec for spec, _ in outs),
        scratch_shapes=list(scratch),
        compiler_params=pltpu.CompilerParams(vmem_limit_bytes=vmem * MIB),
        cost_estimate=pl.CostEstimate(flops=flops, bytes_accessed=moved, transcendentals=0),
    )(*[arg for _, arg in ins])


def col_of(dev, g, pairs, per):
    return pl.multiple_of(((dev % 2 * per + g) * pairs + dev // 2) * HD, HD)


def attend(query_blk, key_blk, value_blk, links, live_count):
    scale = HD ** (-0.5)
    blocks = query_blk.shape[0]
    heads = query_blk.shape[2]
    key_near = key_blk[links].reshape(blocks, NBR * BLK, heads, HD)
    value_near = value_blk[links].reshape(blocks, NBR * BLK, heads, HD)
    scores = (
        jnp.einsum("iqhd,ikhd->hiqk", query_blk, key_near, preferred_element_type=jnp.float32)
        * scale
    )
    live = (jnp.arange(NBR * BLK) // BLK)[None, :] < live_count[:, None]
    scores = jnp.where(live[None, :, None, :], scores, -1e30)
    highest = jnp.max(scores, axis=-1, keepdims=True)
    expo = jnp.exp(scores - highest)
    prob = expo / jnp.sum(expo, axis=-1, keepdims=True)
    prob_bf = prob.astype(jnp.bfloat16)
    attended = jnp.einsum(
        "hiqk,ikhd->iqhd", prob_bf, value_near, preferred_element_type=jnp.float32
    ).astype(jnp.bfloat16)
    return (prob, prob_bf, attended, key_near, value_near)


def backward(query_blk, links, grad_blk, prob, prob_bf, attended, key_near, value_near):
    scale = HD ** (-0.5)
    blocks = query_blk.shape[0]
    heads = query_blk.shape[2]
    value_part = jnp.einsum(
        "hiqk,iqhd->ikhd", prob_bf, grad_blk, preferred_element_type=jnp.float32
    )
    grad_prob = jnp.einsum(
        "iqhd,ikhd->hiqk", grad_blk, value_near, preferred_element_type=jnp.float32
    )
    delta = jnp.einsum("iqhd,iqhd->hiq", grad_blk, attended, preferred_element_type=jnp.float32)
    score_grad = (prob * (grad_prob - delta[..., None]) * scale).astype(jnp.bfloat16)
    query_grad = jnp.einsum(
        "hiqk,ikhd->iqhd", score_grad, key_near, preferred_element_type=jnp.float32
    ).astype(jnp.bfloat16)
    key_part = jnp.einsum(
        "hiqk,iqhd->ikhd", score_grad, query_blk, preferred_element_type=jnp.float32
    )
    member = (links.reshape(-1)[None, :] == jnp.arange(blocks)[:, None]).astype(jnp.float32)
    key_grad = jnp.einsum(
        "ja,aqhd->jqhd",
        member,
        key_part.reshape(blocks * NBR, BLK, heads, HD),
        precision=lax.Precision.HIGHEST,
    )
    value_grad = jnp.einsum(
        "ja,aqhd->jqhd",
        member,
        value_part.reshape(blocks * NBR, BLK, heads, HD),
        precision=lax.Precision.HIGHEST,
    )
    return (query_grad, key_grad.astype(jnp.bfloat16), value_grad.astype(jnp.bfloat16))


def local(queries, key_rows, values, adjacency, counts, out_weight, out_cotangent):
    query_heads, key_heads, value_heads = (
        lax.all_to_all(queries[0], "seq", split_axis=1, concat_axis=0, tiled=True),
        lax.all_to_all(key_rows[0], "seq", split_axis=1, concat_axis=0, tiled=True),
        lax.all_to_all(values[0], "seq", split_axis=1, concat_axis=0, tiled=True),
    )
    length = query_heads.shape[0]
    blocks = length // BLK
    heads = query_heads.shape[1] // HD
    shape = (blocks, BLK, heads, HD)
    links = adjacency[0]
    live_count = counts[0]
    query_blk = query_heads.reshape(shape)
    prob, prob_bf, attended, key_near, value_near = attend(
        query_blk, key_heads.reshape(shape), value_heads.reshape(shape), links, live_count
    )
    attn_tokens = lax.all_to_all(
        attended.reshape(length, heads * HD), "seq", split_axis=0, concat_axis=1, tiled=True
    )
    cotangent = out_cotangent[0]
    columns = attn_tokens
    layer_out = jnp.dot(
        columns,
        lax.all_gather(out_weight, "dp", axis=0, tiled=True),
        preferred_element_type=jnp.float32,
    )
    grad_tokens = lax.dot_general(
        cotangent,
        lax.all_gather(out_weight, "dp", axis=0, tiled=True),
        (((1,), (1,)), ((), ())),
        preferred_element_type=jnp.float32,
    )
    grad_heads = lax.all_to_all(
        grad_tokens.astype(jnp.bfloat16), "seq", split_axis=1, concat_axis=0, tiled=True
    )
    query_grad, key_grad, value_grad = backward(
        query_blk, links, grad_heads.reshape(shape), prob, prob_bf, attended, key_near, value_near
    )
    query_back, key_back, value_back = (
        lax.all_to_all(
            query_grad.reshape(length, heads * HD), "seq", split_axis=0, concat_axis=1, tiled=True
        ),
        lax.all_to_all(
            key_grad.reshape(length, heads * HD), "seq", split_axis=0, concat_axis=1, tiled=True
        ),
        lax.all_to_all(
            value_grad.reshape(length, heads * HD), "seq", split_axis=0, concat_axis=1, tiled=True
        ),
    )
    columns = attn_tokens
    weight_grad = lax.psum_scatter(
        lax.dot_general(
            columns, cotangent, (((0,), (0,)), ((), ())), preferred_element_type=jnp.float32
        ),
        ("dp", "seq"),
        scatter_dimension=0,
        tiled=True,
    )
    return (
        layer_out.astype(jnp.bfloat16)[None],
        query_back[None],
        key_back[None],
        value_back[None],
        weight_grad,
    )


def prep_kernel(n, per, q_ref, k_ref, v_ref, c_ref, w_ref, *rest):
    qkv, (same, other, w_own, whole, sems) = by_slot(rest[:-5], n), rest[-5:]
    s = lax.axis_index("seq")
    core = s % 2
    half = c_ref.shape[2] // 2
    mine = pl.multiple_of(core * half, half)
    theirs = pl.multiple_of((1 - core) * half, half)
    row = pl.multiple_of((s // 2) * HD, HD)
    moves = [(src.at[0], whole.at[t]) for t, src in enumerate((q_ref, k_ref, v_ref))]
    moves.append((c_ref.at[0, :, pl.ds(mine, half)], same))
    moves.append((c_ref.at[0, :, pl.ds(theirs, half)], other))
    moves.append((w_ref.at[pl.ds(row, HD), pl.ds(mine, half)], w_own))
    handles = [pltpu.make_async_copy(src, dst, sems.at[m]) for m, (src, dst) in enumerate(moves)]
    for handle in handles:
        handle.start()
    for t in range(3):
        handles[t].wait()
        for j in range(n):
            for g in range(per):
                col = col_of(s ^ j, g, n // 2, per)
                qkv[j][t, :, g * HD : (g + 1) * HD] = whole[t, :, pl.ds(col, HD)]
    for handle in handles[3:]:
        handle.wait()


def order(n):
    return sorted(range(1, n), key=lambda j: (j == 1, j % 2, -j.bit_count(), j))


def by_slot(refs, n):
    slots = dict(zip([0] + order(n), refs))
    return [slots[j] for j in range(n)]


def stack_kernel(first_ref, second_ref, out_ref):
    rows = first_ref.shape[0]
    out_ref[:rows] = first_ref[...]
    out_ref[rows:] = second_ref[...]


def forward_kernel(n, per, adj_ref, cnt_ref, *rest):
    qkv, rest = by_slot(rest[:-11], n), rest[-11:]
    attn_ref, swap_ref, attn_t_ref, expo, share_ref, queries, keys_t, vals, keys, vals_t, score = rest
    s = lax.axis_index("seq")
    length = n * BLK
    tile = 2 * BLK
    scale = HD**-0.5 * LOG2E
    place = lax.broadcasted_iota(jnp.int32, (n, BLK), 0)
    biases = []
    for i in range(n):
        block = s ^ i
        count = cnt_ref[0, block]
        bias = jnp.full((n, BLK), DEAD, F32)
        for slot in range(NBR):
            j = jnp.where(slot < count, adj_ref[0, block, slot] ^ s, n)
            bias = jnp.where(place == j, 0.0, bias)
        biases.append(bias)
    for g in range(per):
        lanes = slice(g * HD, (g + 1) * HD)
        for j in range(n):
            rows = slice(j * BLK, (j + 1) * BLK)
            queries[g, rows, :] = qkv[j][0, :, lanes]
            key, val = qkv[j][1, :, lanes], qkv[j][2, :, lanes]
            keys[rows, :] = key
            keys_t[g, :, rows] = key.T
            vals[g, rows, :] = val
            vals_t[:, rows] = val.T
        for t in range(length // tile):
            cols = slice(t * tile, (t + 1) * tile)
            bias = jnp.concatenate(biases[2 * t : 2 * t + 2], axis=1)
            query = queries[g, cols, :]
            highest = jnp.full((1, tile), -jnp.inf, F32)
            for j in range(n):
                rows = slice(j * BLK, (j + 1) * BLK)
                part = mm(keys[rows, :], query, NT) * scale + bias[j : j + 1]
                score[rows, :] = part
                highest = jnp.maximum(highest, jnp.max(part, axis=0, keepdims=True))
            total = jnp.zeros((1, tile), F32)
            for j in range(n):
                rows = slice(j * BLK, (j + 1) * BLK)
                part = jnp.exp2(score[rows, :] - highest)
                total = total + jnp.sum(part, axis=0, keepdims=True)
                expo[g, rows, cols] = part.astype(BF16)
            share = 1.0 / total
            share_ref[g : g + 1, cols] = share
            att = (mm(vals_t[...], expo[g, :, cols]) * share).astype(BF16)
            attn_t_ref[g, :, cols] = att
            first, second = att[:, :BLK].T, att[:, BLK:].T
            base = t * tile
            attn_ref[base : base + BLK, lanes] = first
            attn_ref[base + BLK : base + tile, lanes] = second
            swap_ref[base : base + BLK, lanes] = second
            swap_ref[base + BLK : base + tile, lanes] = first


def grow_kernel(bit, mine_ref, recv_ref, out_ref):
    here = lax.axis_index("dp") // bit % 2
    for i in range(mine_ref.shape[0]):
        out_ref[2 * i + here] = mine_ref[i]
        out_ref[2 * i + 1 - here] = recv_ref[i]


def halve(total, bit, keep_ref, send_ref):
    here = lax.axis_index("dp") // bit % 2
    for i in range(keep_ref.shape[0]):
        keep_ref[i] = jnp.where(here == 0, total[2 * i], total[2 * i + 1])
        send_ref[i] = jnp.where(here == 0, total[2 * i + 1], total[2 * i]).astype(BF16)


def fold_kernel(bit, mine_ref, recv_ref, keep_ref, send_ref):
    halve(mine_ref[...] + recv_ref[...].astype(F32), bit, keep_ref, send_ref)


def grad_attn_kernel(n, per, *rest):
    cot, rest = rest[:-4], rest[-4:]
    w_ref, own_ref, send_ref, cot_out = rest
    core = lax.axis_index("seq") % 2
    mine = w_ref[pl.ds(pl.multiple_of(core * per * HD, HD), per * HD), :]
    theirs = w_ref[pl.ds(pl.multiple_of((1 - core) * per * HD, HD), per * HD), :]
    rows = n * BLK // len(cot)
    for j, ref in enumerate(cot):
        cot_out[j * rows : (j + 1) * rows, :] = ref[...]
    for t in range(n // 2):
        base = 2 * t * BLK
        rows = cot_out[base : base + 2 * BLK, :]
        own_ref[:, base : base + 2 * BLK] = mm(mine, rows, NT)
        part = mm(theirs, rows, NT).astype(BF16)
        send_ref[:, base : base + BLK] = part[:, BLK:]
        send_ref[:, base + BLK : base + 2 * BLK] = part[:, :BLK]


def backward_kernel(n, per, expo, share_ref, queries, keys_t, vals, attn_t_ref, own_ref, recv_ref, *rest):
    outs, (dscores,) = by_slot(rest[:-1], n), rest[-1:]
    scale = HD**-0.5
    tile = 4 * BLK
    length = n * BLK
    for g in range(per):
        lanes = slice(g * HD, (g + 1) * HD)
        full = (own_ref[lanes, :] + recv_ref[lanes, :].astype(F32)) * share_ref[g : g + 1, :]
        grad = full.astype(BF16)
        delta = jnp.sum(full * attn_t_ref[g].astype(F32), axis=0, keepdims=True)
        for t in range(length // tile):
            cols = slice(t * tile, (t + 1) * tile)
            dprob = mm(vals[g], grad[:, cols])
            dscores[:, cols] = (expo[g, :, cols].astype(F32) * (dprob - delta[:, cols])).astype(BF16)
        for t in range(length // tile):
            rows = slice(t * tile, (t + 1) * tile)
            dvalue = mm(expo[g, rows, :], grad, NT).astype(BF16)
            dkey = (mm(dscores[rows, :], queries[g]) * scale).astype(BF16)
            dquery = (mm(keys_t[g], dscores[:, rows]).T * scale).astype(BF16)
            for b in range(4):
                part = slice(b * BLK, (b + 1) * BLK)
                outs[4 * t + b][0, :, lanes] = dquery[part]
                outs[4 * t + b][1, :, lanes] = dkey[part]
                outs[4 * t + b][2, :, lanes] = dvalue[part]


def out_kernel(n, attn_ref, recv_ref, w_ref, *outs):
    core = lax.axis_index("seq") % 2
    tile = 2 * BLK
    heads = attn_ref.shape[1]
    mine = w_ref[pl.ds(pl.multiple_of(core * heads, heads), heads), :]
    theirs = w_ref[pl.ds(pl.multiple_of((1 - core) * heads, heads), heads), :]
    for t in range(n // 2):
        rows = slice(t * tile, (t + 1) * tile)
        part = mm(attn_ref[rows, :], mine) + mm(recv_ref[rows, :], theirs)
        if t < 3:
            outs[t][...] = part.astype(outs[t].dtype)
        else:
            outs[3][...] = part[:BLK].astype(BF16)
            outs[4][...] = part[BLK:].astype(BF16)


def relay_kernel(first_ref, first_recv, second_ref, second_recv, *outs):
    outs[0][:BLK] = first_ref[:BLK]
    outs[0][BLK:] = (first_ref[BLK:].astype(F32) + second_recv[...].astype(F32)).astype(BF16)
    outs[1][:BLK] = (second_ref[:BLK].astype(F32) + first_recv[...].astype(F32)).astype(BF16)
    outs[1][BLK:] = second_ref[BLK:]


def weight_kernel(per, attn_t_ref, recv_ref, cot_ref, keep_ref, send_ref, grads):
    core = lax.axis_index("seq") % 2
    for g in range(per):
        grads[core * per + g] = mm(attn_t_ref[g], cot_ref[...])
        recv = recv_ref[:, g * HD : (g + 1) * HD].T
        grads[(1 - core) * per + g] = mm(recv, cot_ref[...])
    halve(grads, 1, keep_ref, send_ref)


def out_sum_kernel(own_ref, *rest):
    parts, (keep_ref, send_ref) = rest[:-2], rest[-2:]
    total = own_ref[...]
    for part in parts:
        total = total + part[...].astype(F32)
    total = total.astype(BF16)
    keep_ref[...] = total[:BLK]
    send_ref[...] = total[BLK:]


def weight_sum_kernel(own_ref, recv_ref, keep_ref, send_ref):
    total = own_ref[0] + recv_ref[0].astype(F32)
    half = total.shape[0] // 2
    core = lax.axis_index("seq") % 2
    keep_ref[...] = jnp.where(core == 0, total[:half], total[half:])
    send_ref[...] = jnp.where(core == 0, total[half:], total[:half])


def place_kernel(n, per, keep_ref, recv_ref, w_keep_ref, w_recv_ref, *rest):
    parts, (out_ref, *outs, w_ref, whole, sems) = by_slot(rest[:-7], n), rest[-7:]
    s = lax.axis_index("seq")
    core = s % 2
    half = keep_ref.shape[1]
    mine = pl.ds(pl.multiple_of(core * half, half), half)
    theirs = pl.ds(pl.multiple_of((1 - core) * half, half), half)
    moves = [
        (keep_ref, out_ref.at[0, :, mine]),
        (recv_ref, out_ref.at[0, :, theirs]),
        (w_keep_ref, w_ref.at[:, mine]),
        (w_recv_ref, w_ref.at[:, theirs]),
    ]
    moves += [(whole.at[t], outs[t].at[0]) for t in range(3)]
    handles = [pltpu.make_async_copy(src, dst, sems.at[m]) for m, (src, dst) in enumerate(moves)]
    for handle in handles[:4]:
        handle.start()
    for t in range(3):
        for j in range(n):
            for g in range(per):
                col = col_of(s ^ j, g, n // 2, per)
                whole[t, :, pl.ds(col, HD)] = parts[j][t, :, g * HD : (g + 1) * HD]
        handles[4 + t].start()
    for handle in handles:
        handle.wait()


def paired(n, nz, queries, key_rows, values, adjacency, counts, out_weight, out_cotangent):
    per = nz // 2
    pairs = n // 2
    length = n * BLK
    wide = queries.shape[2]
    half = wide // 2
    heads = per * HD
    chunk = sds((3, BLK, heads), BF16)
    piece = sds((BLK, half), BF16)
    couple = sds((2 * BLK, half), BF16)

    def to(x, j):
        return lax.ppermute(x, "seq", [(i, i ^ j) for i in range(n)])

    def to_z(x, j):
        return lax.ppermute(x, "dp", [(i, i ^ j) for i in range(nz)])

    def exchange(parts):
        return [parts[0]] + [to(part, j) for part, j in zip(parts[1:], order(n))]

    prep = call(
        functools.partial(prep_kernel, n, per),
        [(HBM, in_hbm(x)) for x in (queries, key_rows, values, out_cotangent, out_weight)],
        [(VMEM, pltpu.VMEM(x.shape, x.dtype)) for x in [chunk] * n + [piece] * 3],
        [pltpu.VMEM((3, BLK, wide), BF16), pltpu.SemaphoreType.DMA((6,))],
        moved=8 * MIB,
    )
    same, other, w_own = prep[n:]
    qkv = exchange(prep[:n])
    (cot_own,) = call(
        stack_kernel, [(VMEM, same), (VMEM, to(other, 1))], [(VMEM, couple)], moved=MIB
    )
    sent = dict(zip(order(n), qkv[1:]))
    cot_sent = after(cot_own, *[sent[j] for j in order(n)[: pairs - 1]])
    cot = [cot_own] + [to(cot_sent, 2 * jc) for jc in range(1, pairs)]
    w_rows = w_own[None]
    bit = nz
    while bit > 1:
        bit //= 2
        (w_rows,) = call(
            functools.partial(grow_kernel, bit),
            [(VMEM, w_rows), (VMEM, to_z(w_rows, bit))],
            [(VMEM, sds((2 * w_rows.shape[0], HD, half), BF16))],
            moved=2 * MIB,
        )
    w_rows = w_rows.reshape(nz * HD, half)

    attn, swap, attn_t, *kept = call(
        functools.partial(forward_kernel, n, per),
        [(SMEM, adjacency), (SMEM, counts)] + [(VMEM, x) for x in qkv],
        [
            (VMEM, sds((length, heads), BF16)),
            (VMEM, sds((length, heads), BF16)),
            (VMEM, sds((per, HD, length), BF16)),
            (VMEM, sds((per, length, length), BF16)),
            (VMEM, sds((per, length), F32)),
            (VMEM, sds((per, length, HD), BF16)),
            (VMEM, sds((per, HD, length), BF16)),
            (VMEM, sds((per, length, HD), BF16)),
        ],
        [
            pltpu.VMEM((length, HD), BF16),
            pltpu.VMEM((HD, length), BF16),
            pltpu.VMEM((length, 2 * BLK), F32),
        ],
        flops=4 * per * length * length * HD,
        moved=8 * MIB,
    )
    attn_recv = to(swap, 1)

    grad_own, grad_send, cot_rows = call(
        functools.partial(grad_attn_kernel, n, per),
        [(VMEM, x) for x in cot + [w_rows]],
        [
            (VMEM, sds((heads, length), F32)),
            (VMEM, sds((heads, length), BF16)),
            (VMEM, sds((length, half), BF16)),
        ],
        flops=4 * length * heads * half,
        moved=8 * MIB,
    )
    grad_recv = to(grad_send, 1)
    out_own, out_x, out_y, out_far_x, out_far_y = call(
        functools.partial(out_kernel, n),
        [(VMEM, attn), (VMEM, attn_recv), (VMEM, after(w_rows, grad_own))],
        [(VMEM, x) for x in (sds((2 * BLK, half), F32), couple, couple, piece, piece)],
        flops=4 * length * heads * half,
        moved=6 * MIB,
    )
    far_x, far_y = to(out_far_x, 2), to(out_far_y, 4)
    w_keep, w_send = call(
        functools.partial(weight_kernel, per),
        [(VMEM, attn_t), (VMEM, attn_recv), (VMEM, cot_rows)],
        [(VMEM, sds((per, HD, half), d)) for d in (F32, BF16)],
        [pltpu.VMEM((nz, HD, half), F32)],
        flops=4 * length * heads * half,
        moved=6 * MIB,
    )
    grads = call(
        functools.partial(backward_kernel, n, per),
        [(VMEM, x) for x in kept + [attn_t, after(grad_own, w_keep, out_own), grad_recv]],
        [(VMEM, chunk)] * n,
        [pltpu.VMEM((length, length), BF16)],
        flops=8 * per * length * length * HD,
        moved=8 * MIB,
    )
    relayed = call(
        relay_kernel,
        [(VMEM, x) for x in (after(out_x, grads[0]), far_x, out_y, far_y)],
        [(VMEM, couple)] * 2,
        moved=3 * MIB,
    )
    out_recv = [to(relayed[0], 2), to(relayed[1], 4)]
    back = exchange(grads)

    bit = 1
    while 2 * bit < nz:
        w_keep, w_send = call(
            functools.partial(fold_kernel, 2 * bit),
            [(VMEM, w_keep), (VMEM, to_z(w_send, bit))],
            [(VMEM, sds((w_keep.shape[0] // 2, HD, half), d)) for d in (F32, BF16)],
            moved=2 * MIB,
        )
        bit *= 2
    w_recv = to_z(w_send, bit)

    out_keep, out_send = call(
        out_sum_kernel,
        [(VMEM, x) for x in [after(out_own, grads[0])] + out_recv],
        [(VMEM, piece)] * 2,
        moved=3 * MIB,
    )
    half_keep, half_send = call(
        weight_sum_kernel,
        [(VMEM, after(w_keep, out_keep, back[1])), (VMEM, w_recv)],
        [(VMEM, sds((HD // 2, half), F32))] * 2,
        moved=2 * MIB,
    )
    token = sds((1, BLK, wide), BF16)
    return call(
        functools.partial(place_kernel, n, per),
        [(VMEM, x) for x in [out_keep, to(out_send, 1), half_keep, to(half_send, 1)] + back],
        [(ANY, token)] * 4 + [(ANY, sds((HD // 2, wide), F32))],
        [pltpu.VMEM((3, BLK, wide), BF16), pltpu.SemaphoreType.DMA((7,))],
        moved=4 * MIB,
    )


def solution(mesh):
    in_specs = (
        P("dp", "seq", None),
        P("dp", "seq", None),
        P("dp", "seq", None),
        P("dp", None, None),
        P("dp", None),
        P("dp", None),
        P("dp", "seq", None),
    )
    out_specs = (
        P("dp", "seq", None),
        P("dp", "seq", None),
        P("dp", "seq", None),
        P("dp", "seq", None),
        P(("dp", "seq"), None),
    )
    n, nz = mesh.shape["seq"], mesh.shape["dp"]

    def body(queries, *rest):
        fits = queries.shape[1] == BLK and queries.shape[2] == nz * (n // 2) * HD
        if fits and n == 8 and nz > 1 and nz & (nz - 1) == 0:
            return paired(n, nz, queries, *rest)
        return local(queries, *rest)

    return jax.shard_map(body, mesh=mesh, in_specs=in_specs, out_specs=out_specs, check_vma=False)
```
